256 devices in a mesh: dp: 32 (over y, z_lo, core), expert: 8 (over z_hi, x).
Axes of the slice: x: 4, y: 4, z: 8 (z_hi: 2, z_lo: 4; z = z_hi * 4 + z_lo), core: 2. Of those that a mesh axis runs over, the one named last changes fastest.
Arguments:
- tokens: bfloat16 [2048, 6144], P(('dp', 'expert')), may hold values from -6 to 6
- routes: int32 [2048, 2], P(('dp', 'expert')), may hold values from 0 to 7, all different within a row; in each aligned block of 8 rows (0 to 7, 8 to 15, ...) at most 3 rows name the same one
- gates: float32 [2048, 2], P(('dp', 'expert')), may hold values from 0.2 to 1
- saved_inputs: bfloat16 [32, 8, 64, 96], P('dp', 'expert'), may hold values from -6 to 6
- cotangents: bfloat16 [32, 8, 64, 2, 8192], P('dp', 'expert'), may hold values from -0.59765625 to 0.59765625
- master: float32 [8, 2, 96, 8192], P('expert', None, 'dp'), may hold values from -0.078125 to 0.078125
- moment: float32 [8, 2, 96, 8192], P('expert', None, 'dp'), may hold values from -3 to 3
- second: float32 [8, 2, 96, 8192], P('expert', None, 'dp'), may hold values from 0.01 to 1
- w_rest: bfloat16 [8, 2, 6048, 8192], P('expert', None, None, 'dp'), may hold values from -0.078125 to 0.078125
- w_down: bfloat16 [8, 6144, 8192], P('expert', None, 'dp'), may hold values from -0.0625 to 0.0625
Outputs:
- mixed: bfloat16 [2048, 6144], P(('dp', 'expert'))
- master_new: float32 [8, 2, 96, 8192], P('expert', None, 'dp')
- moment_new: float32 [8, 2, 96, 8192], P('expert', None, 'dp')
- second_new: float32 [8, 2, 96, 8192], P('expert', None, 'dp')
The draws below stay inside these ranges and needn't reach their ends.
Inputs may be any that keep to these rules, and one draw needn't show every extreme that they name: `routes`: each token names 2 different experts; among the 8 tokens of one device (aligned blocks of rows) no expert is named more than 3 times, a bound that some block reaches.
All inputs are finite; a program needn't handle non-finite values.
Results may differ from the reference program's by a relative error of at most 0.0058.
Values may be sent and summed in bfloat16 or wider, within the bound.
A program may use at most 192 MiB of HBM per device.

```python
import math
import jax
import jax.numpy as jnp
import numpy as np
from jax import lax

D = 6144
HB = 8192
RB = 96
TOK_DEV = 8
GR = 64
TOP = 2
EXPERTS = 8
CAP = 3
REST = 6048
TOKENS = 2048
N_DP = 32


def strengthened(array, key, source, target, parts, factor):
    def block_of(dim):
        return (jnp.arange(array.shape[dim]) // (array.shape[dim] // parts)).reshape((-1,) + (1,) * (array.ndim - 1 - dim))

    one_side = jax.random.permutation(key, parts)[block_of(target)]
    other_side = (block_of(target) + parts // 2) % parts
    return jnp.where((block_of(source) == one_side) | (block_of(source) == other_side), factor * array, array)


def steps_of(key, shape, cuts, smallest, largest):
    level = 1.0
    for axis_at, blocks in cuts:
        heights = jax.random.uniform(jax.random.fold_in(jax.random.fold_in(key, 6), axis_at), (blocks,), jnp.float32, smallest / len(cuts), largest / len(cuts))
        level = level * jnp.repeat(jnp.exp(heights), shape[axis_at] // blocks).reshape((-1,) + (1,) * (len(shape) - 1 - axis_at))
    return level


def shared_out(own_key, own, number, rows, count, top, limit, skew):
    ranking = jax.random.permutation(own_key, count)
    crowded, usual = portions_of(count, rows * top, limit, skew, True), portions_of(count, rows * top, limit, skew, False)
    places = jnp.arange(count)

    def named(lengths, offset_by):
        used = int((lengths > 0).sum())
        fixed = max(1, used // 4)
        shifted = fixed + (places - fixed + offset_by * (used - fixed)) % max(1, count - fixed)
        return jnp.zeros((count,), jnp.int32).at[ranking[jnp.where(places < fixed, places, shifted)]].set(jnp.asarray(lengths, jnp.int32))

    lengths = jnp.where(number % 4 == 0, named(crowded, number // 4), named(usual, number - number // 4 - 1))
    mixed = jax.random.permutation(jax.random.fold_in(own, 3), count)
    source_of, sink = mixed[0:count // 2 * 2:2], mixed[1:count // 2 * 2:2]
    margin = jnp.minimum(lengths[source_of] - 1, limit - lengths[sink]) // 2
    margin = jnp.where((source_of == ranking[0]) | (sink == ranking[0]) | (lengths[sink] == 0), 0, jnp.maximum(margin, 0))
    shifted = jax.random.randint(jax.random.fold_in(own, 4), (count // 2,), 0, 1 << 20) % (margin + 1)
    lengths = lengths.at[source_of].add(-shifted).at[sink].add(shifted)
    labels = jnp.searchsorted(jnp.cumsum(lengths), jnp.arange(rows * top), side="right").astype(jnp.int32)
    listing = labels.reshape(top, rows).T
    listing = listing[jax.random.permutation(jax.random.fold_in(own, 1), rows)]
    offset_by = jax.random.randint(jax.random.fold_in(own, 2), (rows, 1), 0, top)
    return jnp.take_along_axis(listing, (jnp.arange(top)[None, :] + offset_by) % top, axis=1)


def portions_of(number_of, total, limit, skew, full):
    portions = [(1 << 20) // math.isqrt(standing ** skew) + 1 for standing in range(1, number_of + 1)]
    largest = limit if full else min(limit, max(-(-total // number_of), total * portions[0] // sum(portions)))
    least = 1 if total - largest >= number_of - 1 else 0
    given, rest = [largest] + [least] * (number_of - 1), total - largest - least * (number_of - 1)
    while rest > 0:
        movable = [i for i in range(1, number_of) if given[i] < largest] or [i for i in range(1, number_of) if given[i] < limit]
        mass, remaining = sum([portions[i] for i in movable]), rest
        for i in movable:
            addition = min(limit - given[i], max(1, remaining * portions[i] // mass), rest)
            given[i] = given[i] + addition
            rest = rest - addition
    return np.array(given)


def gaussian(stream_key, dims, scale, most, cuts=(), kind=jnp.bfloat16):
    drawn = scale * jax.random.normal(stream_key, dims, jnp.float32)
    if cuts:
        drawn = drawn * steps_of(stream_key, dims, cuts, -0.22, 0.18)
    return jnp.clip(drawn, -most, most).astype(kind)


def heavy_noise(stream_key, extent, deviation, most, shards, heavy, kind=jnp.bfloat16):
    values = deviation * jax.random.normal(stream_key, extent, jnp.float32)
    if shards:
        values = values * steps_of(stream_key, extent, shards, -0.22, 0.18)
    return jnp.clip(strengthened(values, jax.random.fold_in(stream_key, 3), *heavy), -most, most).astype(kind)


def setup_inputs(seed: int = 0) -> dict:
    arg_keys = jax.random.split(jax.random.key(seed), 11)
    tokens = gaussian(arg_keys[0], (TOKENS, D), 1.0, 6.0, ((0, 256),))
    routes_keys = jax.random.split(jax.random.fold_in(arg_keys[1], 1), TOKENS // TOK_DEV)
    routes_turns = jax.random.permutation(jax.random.fold_in(arg_keys[1], 3), TOKENS // TOK_DEV)
    routes = jax.vmap(lambda own, number: shared_out(jax.random.fold_in(arg_keys[1], 2), own, number, TOK_DEV, EXPERTS, TOP, CAP, 1))(routes_keys, routes_turns).reshape((TOKENS, TOP))
    gates = jnp.clip(0.2 + 0.8 * jax.random.uniform(arg_keys[2], (TOKENS, TOP), jnp.float32) ** steps_of(arg_keys[2], (TOKENS, TOP), ((0, 256),), -0.2, 0.2), 0.2, 1.0)
    saved_inputs = heavy_noise(arg_keys[3], (N_DP, EXPERTS, GR, RB), 1.0, 6.0, ((0, 32), (1, 8)), (0, 3, 32, 2.75))
    cotangents = gaussian(arg_keys[4], (N_DP, EXPERTS, GR, 2, HB), 0.1, 0.59765625, ((0, 32), (1, 8)))
    master = gaussian(arg_keys[5], (EXPERTS, 2, RB, HB), D ** -0.5, 0.078125, ((0, 8), (2, 32)), jnp.float32)
    moment = gaussian(arg_keys[6], (EXPERTS, 2, RB, HB), 0.5, 3.0, ((0, 8), (2, 32)), jnp.float32)
    second = jnp.clip(jnp.exp(math.log(1.0) - 4.6051702 * jax.random.uniform(arg_keys[7], (EXPERTS, 2, RB, HB), jnp.float32) ** steps_of(arg_keys[7], (EXPERTS, 2, RB, HB), ((0, 8), (2, 32)), -0.2, 0.2)), 0.01, 1.0)
    w_rest = gaussian(arg_keys[8], (EXPERTS, 2, REST, HB), D ** -0.5, 0.078125, ((0, 8), (3, 32)))
    w_down = gaussian(arg_keys[9], (EXPERTS, D, HB), HB ** -0.5, 0.0625, ((0, 8), (2, 32)))
    return {"tokens": tokens, "routes": routes, "gates": gates, "saved_inputs": saved_inputs, "cotangents": cotangents, "master": master, "moment": moment, "second": second, "w_rest": w_rest, "w_down": w_down}


beta_one = 0.9
beta_two = 0.999
rate = 0.01
epsilon = 1e-08
bias_one = 1.0 - 0.9 ** 20
bias_two = 1.0 - 0.999 ** 20

def dispatch(rows, picks, experts, cap):
    flat = picks.reshape(-1).astype(jnp.int32)
    count = flat.shape[0]
    onehot = (flat[:, None] == jnp.arange(experts, dtype=jnp.int32)[None, :]).astype(jnp.int32)
    before = jnp.cumsum(onehot, axis=0, dtype=jnp.int32) - onehot
    slot = lax.optimization_barrier(jnp.sum(before * onehot, axis=1)).astype(jnp.int32)
    target = (flat * cap + slot).astype(jnp.int32)
    source = (jnp.arange(count, dtype=jnp.int32) // picks.shape[1]).astype(jnp.int32)
    table = jnp.full((experts * cap,), rows.shape[0], jnp.int32).at[target].set(source)
    padded = jnp.concatenate([rows, jnp.zeros((1, rows.shape[1]), rows.dtype)], axis=0)
    buffer = padded[table].reshape(experts, cap, rows.shape[1])
    return (buffer, target)

def combine(results, target, gates):
    flat = results.reshape(-1, results.shape[-1])
    picked = flat[target].astype(jnp.float32).reshape(gates.shape[0], gates.shape[1], -1)
    return lax.optimization_barrier(jnp.sum(picked * gates[:, :, None], axis=1)).astype(jnp.bfloat16)

def reference(tokens, routes, gates, saved_inputs, cotangents, master, moment, second, w_rest, w_down):

    def expert_gradient(item):
        inputs, backs = item
        return jnp.einsum('pgr,pgmh->mrh', inputs.astype(jnp.float32), backs.astype(jnp.float32))
    gradient = lax.map(expert_gradient, (jnp.swapaxes(saved_inputs, 0, 1), jnp.swapaxes(cotangents, 0, 1)))
    moment_new = beta_one * moment + (1.0 - beta_one) * gradient
    second_new = beta_two * second + (1.0 - beta_two) * gradient * gradient
    master_new = master - rate * (moment_new / bias_one) / (jnp.sqrt(second_new / bias_two) + epsilon)
    bucket = master_new.astype(jnp.bfloat16)
    gate_up = jnp.concatenate([bucket, w_rest], axis=2)
    blocks = TOKENS // TOK_DEV

    def place(rows, picks):
        return dispatch(rows, picks, EXPERTS, CAP)
    buffers, targets = jax.vmap(place)(tokens.reshape(blocks, TOK_DEV, D), routes.reshape(blocks, TOK_DEV, TOP))

    def one_expert(item):
        rows_in, weights, down = item
        flat = rows_in.reshape(-1, D).astype(jnp.float32)
        gate = jnp.dot(flat, weights[0].astype(jnp.float32))
        up = jnp.dot(flat, weights[1].astype(jnp.float32))
        hidden_low = lax.optimization_barrier((jax.nn.silu(gate) * up).astype(jnp.bfloat16))
        total = jnp.dot(hidden_low.astype(jnp.float32), down.astype(jnp.float32).T)
        return total.astype(jnp.bfloat16).reshape(rows_in.shape)
    outputs = lax.map(one_expert, (jnp.swapaxes(buffers, 0, 1), gate_up, w_down))
    results = jnp.swapaxes(outputs, 0, 1)
    mixed = jax.vmap(combine)(results, targets, gates.reshape(blocks, TOK_DEV, TOP))
    return (mixed.reshape(TOKENS, D), master_new, moment_new, second_new)
```

```python
import jax
import jax.numpy as jnp
from jax import lax
from jax.experimental import pallas as pl
from jax.experimental.pallas import tpu as pltpu
from jax.sharding import PartitionSpec as P

beta_one = 0.9
beta_two = 0.999
rate = 0.01
epsilon = 1e-08
bias_one = 1.0 - 0.9**20
bias_two = 1.0 - 0.999**20

BF = jnp.bfloat16
F32 = jnp.float32
MESH = pl.DeviceIdType.MESH
D = 6144
HALF = 3072
UNITS = 256
ROWS = 48
DZ = (0, 1, 3, 2)
SLOT = (0, 1, 3, 2)
N_SEND = 96


def kernel(
    tokens, routes, gates, saved, cot, master, moment, second, w_rest, w_down,
    mixed, master_new, moment_new, second_new,
    tok_half, tok_pair, meta_own, meta_sib, meta_all, toks,
    saved_sib, saved_t, cots, pg, g_opp, g_fin, zg, zg_in, grad_out, grad, bucket_out, bucket_in,
    w, wd, pick, x, hid, acc, po, r_opp, r_fin, rz, z_out, ct, rx, zh_out, zh_in, fin, fin_in,
    ssem, lsem, s_pair, s_tok, s_meta, s_x, s_xs, s_gopp, s_gfin, s_zg,
    s_ga, s_gb, s_ba, s_bb, s_hid, s_ropp, s_rfin, s_rz, s_rx, s_fin,
):
    dp = lax.axis_index("dp")
    ex = lax.axis_index("expert")
    y, z, c = dp // 8, (dp // 2) % 4, dp % 2
    zh, xx = ex // 4, ex % 4
    oc = 1 - c

    def at(dy, dz, core):
        return (((y + dy) % 4) * 8 + ((z + dz) % 4) * 2 + core, ex)

    sib = at(0, 0, oc)
    opp_e = (dp, (1 - zh) * 4 + xx)

    def along_x(d):
        return (dp, zh * 4 + (xx + d) % 4)

    sends = []

    def send(src, dst, rsem, dev):
        d = pltpu.make_async_remote_copy(
            src_ref=src, dst_ref=dst, send_sem=ssem.at[len(sends)], recv_sem=rsem,
            device_id=dev, device_id_type=MESH,
        )
        d.start()
        sends.append(d)

    def got(dst, rsem):
        pltpu.make_async_remote_copy(
            src_ref=dst, dst_ref=dst, send_sem=ssem.at[0], recv_sem=rsem,
            device_id=sib, device_id_type=MESH,
        ).wait_recv()

    bar = pltpu.get_barrier_semaphore()

    def greet(s, carry):
        pl.semaphore_signal(bar, inc=1, device_id=((dp + s) % 32, ex), device_id_type=MESH)
        return carry

    lax.fori_loop(1, 32, greet, 0)
    for dev in (opp_e, along_x(1), along_x(2), along_x(3)):
        pl.semaphore_signal(bar, inc=1, device_id=dev, device_id_type=MESH)

    local = [
        pltpu.make_async_copy(cot.at[c], cots.at[:, pl.ds(0, 64)], lsem.at[0]),
        pltpu.make_async_copy(w_rest, w.at[:, pl.ds(96, 6048)], lsem.at[1]),
        pltpu.make_async_copy(w_down.at[pl.ds(c * HALF, HALF)], wd.at[0], lsem.at[2]),
    ]
    for d in local:
        d.start()
    tok_half[0] = tokens[:, :HALF].astype(F32)
    tok_half[1] = tokens[:, HALF:].astype(F32)
    lane = lax.broadcasted_iota(jnp.int32, (2, 128), 1)
    base = ex * 16 + c * 8
    route_row = jnp.zeros((2, 128), F32)
    gate_row = jnp.zeros((2, 128), F32)
    for t in range(8):
        here = lane == base + t
        route_row = jnp.where(here, routes[:, t : t + 1].astype(F32), route_row)
        gate_row = jnp.where(here, gates[:, t : t + 1], gate_row)
    meta_own[...] = jnp.zeros((8, 128), F32)
    meta_own[0:2, :] = route_row
    meta_own[2:4, :] = gate_row

    pl.semaphore_wait(bar, 35)

    send(tok_half.at[oc], tok_pair.at[c], s_pair.at[0], sib)
    send(meta_own, meta_sib, s_pair.at[1], sib)
    send(saved, saved_sib, s_pair.at[2], sib)
    send(cot.at[oc], cots.at[:, pl.ds(64, 64)], s_pair.at[3], sib)
    send(w_down.at[pl.ds(oc * HALF, HALF)], wd.at[1], s_pair.at[4], sib)

    tok_pair[c] = tok_half[c]
    got(tok_pair.at[oc], s_pair.at[0])
    got(meta_sib, s_pair.at[1])
    toks[ex] = tok_pair[...].reshape(16, HALF).astype(BF)
    meta_all[ex] = meta_own[...] + meta_sib[...]
    send(toks.at[ex], toks.at[ex], s_tok.at[1, 0], opp_e)
    send(meta_all.at[ex], meta_all.at[ex], s_meta.at[1, 0], opp_e)
    for d in (1, 3, 2):
        send(toks.at[ex], toks.at[ex], s_tok.at[0, (4 - d) % 4], along_x(d))
        send(meta_all.at[ex], meta_all.at[ex], s_meta.at[0, (4 - d) % 4], along_x(d))

    got(saved_sib, s_pair.at[2])
    saved_t[...] = jnp.transpose(
        jnp.concatenate([saved[...].astype(F32), saved_sib[...].astype(F32)], axis=0)
    ).astype(BF)
    local[0].wait()
    got(cots.at[:, pl.ds(64, 64)], s_pair.at[3])
    for dy in (2, 1, 3, 0):
        block = cots.at[(y + dy) % 4]
        for h in range(2):
            pg[dy, h] = jnp.dot(
                saved_t[...], block[:, h * 1024 : (h + 1) * 1024], preferred_element_type=F32
            ).astype(BF)
        if dy == 2:
            send(pg.at[2, 0], g_opp.at[0], s_gopp.at[0], at(3, 0, c))
            send(pg.at[2, 1], g_opp.at[1], s_gopp.at[1], at(1, 0, c))
        if dy == 1:
            send(pg.at[1, 0], g_fin.at[0, 0], s_gfin.at[0, 0], at(1, 0, c))
        if dy == 3:
            send(pg.at[3, 1], g_fin.at[1, 1], s_gfin.at[1, 1], at(3, 0, c))

    other = (1 - zh) * 4 + xx
    got(toks.at[other], s_tok.at[1, 0])
    got(meta_all.at[other], s_meta.at[1, 0])
    for d in (1, 3, 2):
        send(toks.at[other], toks.at[other], s_tok.at[1, (4 - d) % 4], along_x(d))
        send(meta_all.at[other], meta_all.at[other], s_meta.at[1, (4 - d) % 4], along_x(d))

    got(g_opp.at[0], s_gopp.at[0])
    pg[3, 0] = (pg[3, 0].astype(F32) + g_opp[0].astype(F32)).astype(BF)
    send(pg.at[3, 0], g_fin.at[1, 0], s_gfin.at[1, 0], at(3, 0, c))
    got(g_opp.at[1], s_gopp.at[1])
    pg[1, 1] = (pg[1, 1].astype(F32) + g_opp[1].astype(F32)).astype(BF)
    send(pg.at[1, 1], g_fin.at[0, 1], s_gfin.at[0, 1], at(1, 0, c))

    for d in (1, 3, 2):
        for k in range(2):
            src = (zh if k == 0 else 1 - zh) * 4 + (xx + d) % 4
            got(toks.at[src], s_tok.at[k, d])
            got(meta_all.at[src], s_meta.at[k, d])
    meta = meta_all[0]
    for e in range(1, 8):
        meta = meta + meta_all[e]
    mine = ex.astype(F32)
    first = meta[0:1, :] == mine
    hit = jnp.logical_or(first, meta[1:2, :] == mine)
    hit_f = jnp.where(hit, 1.0, 0.0).astype(F32)
    gate_of = jnp.where(first, meta[2:3, :], meta[3:4, :])
    before = jnp.where(
        lax.broadcasted_iota(jnp.int32, (128, 128), 0)
        < lax.broadcasted_iota(jnp.int32, (128, 128), 1),
        1.0,
        0.0,
    ).astype(BF)
    rank = jnp.dot(
        jnp.broadcast_to(hit_f, (16, 128)).astype(BF), before, preferred_element_type=F32
    )[0:1, :]
    slot_id = lax.broadcasted_iota(jnp.int32, (ROWS, 128), 0).astype(F32)
    chosen = jnp.where(slot_id == rank, 1.0, 0.0).astype(F32) * hit_f
    row_gate = jnp.sum(chosen * gate_of, axis=1, keepdims=True)
    pick[0] = chosen
    pick[1] = jnp.broadcast_to(row_gate, (ROWS, 128))
    for e in range(6):
        cols = slice(e * 512, (e + 1) * 512)
        x[0, 0, 0, :, cols] = jnp.dot(
            chosen.astype(BF), toks[:, :, cols].reshape(128, 512), preferred_element_type=F32
        ).astype(BF)

    def pass_block(dy, s, y_sides):
        for side in y_sides:
            dst_dy = (dy - side) % 4
            send(x.at[0, dy, s], x.at[0, dst_dy, s], s_x.at[dst_dy, s], at(side, 0, c))
        send(x.at[0, dy, s], x.at[1, dy, s], s_xs.at[dy, s], sib)

    for s in (1, 2, 3):
        t = SLOT[(4 - DZ[s]) % 4]
        send(x.at[0, 0, 0], x.at[0, 0, t], s_x.at[0, t], at(0, DZ[s], c))
    pass_block(0, 0, (1, 3))

    for h in range(2):
        got(g_fin.at[0, h], s_gfin.at[0, h])
        got(g_fin.at[1, h], s_gfin.at[1, h])
        total = pg[0, h].astype(F32) + g_fin[0, h].astype(F32) + g_fin[1, h].astype(F32)
        zg[2 * h] = total[:, :512].astype(BF)
        zg[2 * h + 1] = total[:, 512:].astype(BF)
    for d in (1, 3, 2):
        send(zg.at[(z + d) % 4], zg_in.at[3 - d], s_zg.at[3 - d], at(0, d, c))

    for s in (1, 2, 3):
        got(x.at[0, 0, s], s_x.at[0, s])
        pass_block(0, s, (1, 3))

    full = zg[z].astype(F32)
    for d in range(3):
        got(zg_in.at[d], s_zg.at[d])
        full = full + zg_in[d].astype(F32)
    grad_out[:, 0:1, :] = full[:, :UNITS].reshape(96, 1, UNITS)
    grad_out[:, 1:2, :] = full[:, UNITS:].reshape(96, 1, UNITS)

    def my_columns(p):
        return pl.ds(pl.multiple_of(p * UNITS, UNITS), UNITS)

    def exchange(src_of, dst_of, wait_of, out_sem, in_sem):
        def copy_to(s):
            p = (dp + s) % 32
            return pltpu.make_async_remote_copy(
                src_ref=src_of(p), dst_ref=dst_of(dp), send_sem=out_sem.at[s],
                recv_sem=in_sem.at[dp], device_id=(p, ex), device_id_type=MESH,
            )

        def start(s, carry):
            copy_to(s).start()
            return carry

        def finish(s, carry):
            p = (dp + s) % 32
            pltpu.make_async_remote_copy(
                src_ref=src_of(p), dst_ref=dst_of(p), send_sem=out_sem.at[s],
                recv_sem=in_sem.at[p], device_id=(p, ex), device_id_type=MESH,
            ).wait_recv()
            return carry

        def sent(s, carry):
            copy_to(s).wait_send()
            return carry

        def begin():
            pltpu.make_async_copy(src_of(dp), dst_of(dp), lsem.at[wait_of]).start()
            lax.fori_loop(1, 32, start, 0)

        def arrive():
            pltpu.make_async_copy(src_of(dp), dst_of(dp), lsem.at[wait_of]).wait()
            lax.fori_loop(1, 32, finish, 0)

        return begin, arrive, lambda: lax.fori_loop(1, 32, sent, 0)

    to_rows, rows_here, rows_sent = exchange(
        lambda p: grad_out.at[pl.ds(p * 3, 3)], lambda p: grad.at[:, :, my_columns(p)],
        3, s_ga, s_gb,
    )
    to_cols, cols_here, cols_sent = exchange(
        lambda p: bucket_out.at[:, :, my_columns(p)], lambda p: bucket_in.at[pl.ds(p * 3, 3)],
        4, s_ba, s_bb,
    )
    to_rows()

    for s in (0, 1):
        got(x.at[0, 3, s], s_x.at[3, s])
        pass_block(3, s, (1,))
        got(x.at[0, 1, s], s_x.at[1, s])
        pass_block(1, s, ())

    rows_here()

    def adam(k, carry):
        cols = pl.ds(pl.multiple_of(k * 1024, 1024), 1024)
        g = grad[:, :, cols]
        mo = beta_one * moment[:, :, cols] + (1.0 - beta_one) * g
        se = beta_two * second[:, :, cols] + (1.0 - beta_two) * g * g
        ma = master[:, :, cols] - rate * (mo / bias_one) / (jnp.sqrt(se / bias_two) + epsilon)
        moment_new[:, :, cols] = mo
        second_new[:, :, cols] = se
        master_new[:, :, cols] = ma
        bucket_out[:, :, cols] = ma.astype(BF).astype(F32)
        return carry

    lax.fori_loop(0, 8, adam, 0)
    to_cols()

    for s in (2, 3):
        got(x.at[0, 1, s], s_x.at[1, s])
        pass_block(1, s, (3,))
        got(x.at[0, 3, s], s_x.at[3, s])
        pass_block(3, s, ())

    local[1].wait()
    cols_here()
    for m in range(2):
        w[m, 0:96, :] = bucket_in[:, m : m + 1, :].reshape(96, UNITS).astype(BF)

    def gate_up(dy, s0, ns):
        rows = ns * ROWS
        for hr in range(2):
            start = (c if hr == 0 else oc) * HALF

            def step(k, carry):
                off = pl.multiple_of(k * 1024, 1024)
                left = x[hr, dy, s0 : s0 + ns, :, pl.ds(off, 1024)].reshape(rows, 1024)
                deep = pl.ds(pl.multiple_of(start + off, 1024), 1024)
                for m in range(2):
                    part = jnp.dot(left, w[m, deep, :], preferred_element_type=F32)
                    acc[m, 0:rows] = acc[m, 0:rows] + part
                return carry

            if hr == 0:
                acc[:, 0:rows] = jnp.zeros((2, rows, UNITS), F32)
            lax.fori_loop(0, 3, step, 0)
        gate = acc[0, 0:rows]
        hidden = gate / (1.0 + jnp.exp(-gate)) * acc[1, 0:rows]
        hid[0, dy, s0 : s0 + ns] = hidden.astype(BF).reshape(ns, ROWS, UNITS)
        send(
            hid.at[0, dy, pl.ds(s0, ns)], hid.at[1, dy, pl.ds(s0, ns)],
            s_hid.at[dy, 0 if s0 == 0 else 1], sib,
        )

    def down(dy, s0, ns):
        rows = ns * ROWS
        got(hid.at[1, dy, pl.ds(s0, ns)], s_hid.at[dy, 0 if s0 == 0 else 1])
        one = hid[0, dy, s0 : s0 + ns].reshape(rows, UNITS)
        two = hid[1, dy, s0 : s0 + ns].reshape(rows, UNITS)
        nt = (((1,), (1,)), ((), ()))

        def step(k, carry):
            cols = pl.ds(pl.multiple_of(k * 512, 512), 512)
            out = lax.dot_general(one, wd[0, cols, :], nt, preferred_element_type=F32)
            out = out + lax.dot_general(two, wd[1, cols, :], nt, preferred_element_type=F32)
            po[dy, s0 : s0 + ns, :, cols] = out.astype(BF).reshape(ns, ROWS, 512)
            return carry

        lax.fori_loop(0, 6, step, 0)

    def sibling_rows(dy, s0, ns):
        for s in range(s0, s0 + ns):
            got(x.at[1, dy, s], s_xs.at[dy, s])

    A, B = pl.ds(0, 2), pl.ds(2, 2)
    sibling_rows(0, 0, 4)
    gate_up(0, 0, 4)
    sibling_rows(1, 0, 4)
    gate_up(1, 0, 4)
    sibling_rows(3, 0, 4)
    gate_up(3, 0, 4)
    local[2].wait()
    got(wd.at[1], s_pair.at[4])
    down(1, 0, 4)
    send(po.at[1, A], r_fin.at[0, A], s_rfin.at[0, 0], at(1, 0, c))
    down(3, 0, 4)
    send(po.at[3, B], r_fin.at[1, B], s_rfin.at[1, 1], at(3, 0, c))
    for s in (0, 1):
        got(x.at[0, 2, s], s_x.at[2, s])
        pass_block(2, s, ())
        got(x.at[0, 2, s + 2], s_x.at[2, s + 2])
        pass_block(2, s + 2, ())
    sibling_rows(2, 0, 2)
    gate_up(2, 0, 2)
    sibling_rows(2, 2, 2)
    gate_up(2, 2, 2)
    down(2, 0, 2)
    send(po.at[2, A], r_opp.at[0], s_ropp.at[0], at(3, 0, c))
    down(2, 2, 2)
    send(po.at[2, B], r_opp.at[1], s_ropp.at[1], at(1, 0, c))
    down(0, 0, 4)

    def add_opposite(dy, s0, h):
        def step(k, carry):
            cols = pl.ds(pl.multiple_of(k * 512, 512), 512)
            mine_here = po[dy, s0 : s0 + 2, :, cols].astype(F32)
            po[dy, s0 : s0 + 2, :, cols] = (
                mine_here + r_opp[h, :, :, cols].astype(F32)
            ).astype(BF)
            return carry

        lax.fori_loop(0, 6, step, 0)

    got(r_opp.at[0], s_ropp.at[0])
    add_opposite(3, 0, 0)
    send(po.at[3, A], r_fin.at[1, A], s_rfin.at[1, 0], at(3, 0, c))
    got(r_opp.at[1], s_ropp.at[1])
    add_opposite(1, 2, 1)
    send(po.at[1, B], r_fin.at[0, B], s_rfin.at[0, 1], at(1, 0, c))

    got(r_fin.at[0, A], s_rfin.at[0, 0])
    got(r_fin.at[1, B], s_rfin.at[1, 1])

    def y_sum(s):
        def step(k, carry):
            cols = pl.ds(pl.multiple_of(k * 512, 512), 512)
            total = po[0, s, :, cols].astype(F32) + r_fin[0, s, :, cols].astype(F32)
            z_out[s, :, cols] = (total + r_fin[1, s, :, cols].astype(F32)).astype(BF)
            return carry

        lax.fori_loop(0, 6, step, 0)
        if s > 0:
            send(z_out.at[s], rz.at[SLOT[(4 - DZ[s]) % 4] - 1], s_rz.at[SLOT[(4 - DZ[s]) % 4] - 1], at(0, DZ[s], c))

    got(r_fin.at[1, A], s_rfin.at[1, 0])
    y_sum(1)
    got(r_fin.at[0, B], s_rfin.at[0, 1])
    y_sum(3)
    y_sum(2)
    y_sum(0)
    for s in range(3):
        got(rz.at[s], s_rz.at[s])

    chosen_b = pick[0].astype(BF)
    gate_b = pick[1][:, 0:1]
    for k in range(6):
        cols = slice(k * 512, (k + 1) * 512)
        total = z_out[0, :, cols].astype(F32)
        for s in range(3):
            total = total + rz[s, :, cols].astype(F32)
        scaled = (total * gate_b).astype(BF)
        placed = lax.dot_general(
            chosen_b, scaled, (((0,), (0,)), ((), ())), preferred_element_type=F32
        )
        ct[:, :, :, cols] = placed.astype(BF).reshape(2, 4, 16, 512)
    for d in (1, 3, 2):
        send(ct.at[:, (xx + d) % 4], rx.at[3 - d], s_rx.at[3 - d], along_x(d))
    for d in range(3):
        got(rx.at[d], s_rx.at[d])

    def x_sum(which):
        total = ct[which, xx].astype(F32)
        for d in range(3):
            total = total + rx[d, which].astype(F32)
        return total

    zh_out[...] = x_sum(1 - zh).astype(BF)
    send(zh_out, zh_in, s_fin.at[0], opp_e)
    own = x_sum(zh)
    got(zh_in, s_fin.at[0])
    fin[...] = (own + zh_in[...].astype(F32)).reshape(2, 8, HALF)
    send(fin.at[oc], fin_in, s_fin.at[1], sib)
    mixed[:, pl.ds(pl.multiple_of(c * HALF, HALF), HALF)] = fin[c].astype(BF)
    got(fin_in, s_fin.at[1])
    mixed[:, pl.ds(pl.multiple_of(oc * HALF, HALF), HALF)] = fin_in[...].astype(BF)

    for d in sends:
        d.wait_send()
    rows_sent()
    cols_sent()


def body(tokens, routes, gates, saved_inputs, cotangents, master, moment, second, w_rest, w_down):
    cot = cotangents[0, 0].reshape(64, 2, 4, 4, 2, UNITS)
    cot = jnp.transpose(cot, (4, 2, 0, 3, 1, 5)).reshape(2, 4, 64, 2048)
    rows = [jnp.swapaxes(a[0], 0, 1) for a in (master, moment, second)]
    state = jax.ShapeDtypeStruct((3, 2, 8192), F32)
    vmem = pl.BlockSpec(memory_space=pltpu.VMEM)
    hbm = pl.BlockSpec(memory_space=pl.ANY)
    dma = pltpu.SemaphoreType.DMA
    V = pltpu.VMEM
    out = pl.pallas_call(
        kernel,
        out_shape=(jax.ShapeDtypeStruct((8, D), BF), state, state, state),
        in_specs=[vmem, vmem, vmem, vmem, hbm, vmem, vmem, vmem, hbm, hbm],
        out_specs=(vmem, vmem, vmem, vmem),
        scratch_shapes=[
            V((2, 8, HALF), F32),
            V((2, 8, HALF), F32),
            V((8, 128), F32),
            V((8, 128), F32),
            V((8, 8, 128), F32),
            V((8, 16, HALF), BF),
            V((64, 96), BF),
            V((96, 128), BF),
            V((4, 128, 2048), BF),
            V((4, 2, 96, 1024), BF),
            V((2, 96, 1024), BF),
            V((2, 2, 96, 1024), BF),
            V((4, 96, 512), BF),
            V((3, 96, 512), BF),
            V((96, 2, UNITS), F32),
            V((3, 2, 8192), F32),
            V((3, 2, 8192), F32),
            V((96, 2, UNITS), F32),
            V((2, D, UNITS), BF),
            V((2, HALF, UNITS), BF),
            V((2, ROWS, 128), F32),
            V((2, 4, 4, ROWS, HALF), BF),
            V((2, 4, 4, ROWS, UNITS), BF),
            V((2, 4 * ROWS, UNITS), F32),
            V((4, 4, ROWS, HALF), BF),
            V((2, 2, ROWS, HALF), BF),
            V((2, 4, ROWS, HALF), BF),
            V((3, ROWS, HALF), BF),
            V((4, ROWS, HALF), BF),
            V((2, 4, 16, HALF), BF),
            V((3, 2, 16, HALF), BF),
            V((16, HALF), BF),
            V((16, HALF), BF),
            V((2, 8, HALF), F32),
            V((8, HALF), F32),
            dma((N_SEND,)), dma((5,)), dma((5,)), dma((2, 4)), dma((2, 4)),
            dma((4, 4)), dma((4, 4)), dma((2,)), dma((2, 2)), dma((3,)),
            dma((32,)), dma((32,)), dma((32,)), dma((32,)),
            dma((4, 2)), dma((2,)), dma((2, 2)), dma((3,)), dma((3,)), dma((2,)),
        ],
        compiler_params=pltpu.CompilerParams(
            collective_id=0, has_side_effects=True, vmem_limit_bytes=60 * 1024 * 1024
        ),
        cost_estimate=pl.CostEstimate(flops=8 * 10**9, bytes_accessed=12 * 10**6, transcendentals=0),
    )(
        tokens, jnp.transpose(routes), jnp.transpose(gates), saved_inputs[0, 0], cot, *rows,
        w_rest[0], w_down[0],
    )
    states = [jnp.swapaxes(a, 0, 1)[None] for a in out[1:]]
    return (out[0], *states)


def solution(mesh):
    in_specs = (
        P(("dp", "expert"), None),
        P(("dp", "expert"), None),
        P(("dp", "expert"), None),
        P("dp", "expert", None, None),
        P("dp", "expert", None, None, None),
        P("expert", None, "dp", None),
        P("expert", None, "dp", None),
        P("expert", None, "dp", None),
        P("expert", None, None, "dp"),
        P("expert", None, "dp"),
    )
    out_specs = (
        P(("dp", "expert"), None),
        P("expert", None, "dp", None),
        P("expert", None, "dp", None),
        P("expert", None, "dp", None),
    )
    return jax.shard_map(body, mesh=mesh, in_specs=in_specs, out_specs=out_specs, check_vma=False)
```

```python
import jax
import jax.numpy as jnp
from jax import lax
from jax.experimental import pallas as pl
from jax.experimental.pallas import tpu as pltpu
from jax.sharding import PartitionSpec as P

beta_one = 0.9
beta_two = 0.999
rate = 0.01
epsilon = 1e-08
bias_one = 1.0 - 0.9**20
bias_two = 1.0 - 0.999**20

BF = jnp.bfloat16
F32 = jnp.float32
MESH = pl.DeviceIdType.MESH
D = 6144
HALF = 3072
UNITS = 256
ROWS = 48
DZ = (0, 1, 3, 2)
SLOT = (0, 1, 3, 2)
N_SEND = 190
Q = 3
W = HALF // Q


def kernel(
    tokens, routes, gates, saved, cot, master, moment, second, w_rest, w_down,
    mixed, grad_new,
    tok_half, tok_pair, meta_own, meta_sib, meta_all, toks,
    saved_sib, saved_t, cots, pg, g_opp, g_fin, zg, zg_in, grad_out, grad, bucket_out, bucket_in,
    w, wd, pick, x, hid, acc, po, r_opp, r_fin, rz, z_own, z_out, ct, rx, zh_out, zh_in, fin, fin_in,
    ssem, lsem, s_pair, s_tok, s_meta, s_x, s_xs, s_gopp, s_gfin, s_zg,
    s_ga, s_gb, s_ba, s_bb, s_hid, s_ropp, s_rfin, s_rz, s_rx, s_zh, s_fin,
):
    dp = lax.axis_index("dp")
    ex = lax.axis_index("expert")
    y, z, c = dp // 8, (dp // 2) % 4, dp % 2
    zh, xx = ex // 4, ex % 4
    oc = 1 - c

    def at(dy, dz, core):
        return (((y + dy) % 4) * 8 + ((z + dz) % 4) * 2 + core, ex)

    sib = at(0, 0, oc)
    opp_e = (dp, (1 - zh) * 4 + xx)

    def along_x(d):
        return (dp, zh * 4 + (xx + d) % 4)

    sends = []

    def send(src, dst, rsem, dev):
        d = pltpu.make_async_remote_copy(
            src_ref=src, dst_ref=dst, send_sem=ssem.at[len(sends)], recv_sem=rsem,
            device_id=dev, device_id_type=MESH,
        )
        d.start()
        sends.append(d)

    def got(dst, rsem):
        pltpu.make_async_remote_copy(
            src_ref=dst, dst_ref=dst, send_sem=ssem.at[0], recv_sem=rsem,
            device_id=sib, device_id_type=MESH,
        ).wait_recv()

    bar = pltpu.get_barrier_semaphore()

    def greet(s, carry):
        pl.semaphore_signal(bar, inc=1, device_id=((dp + s) % 32, ex), device_id_type=MESH)
        return carry

    lax.fori_loop(1, 32, greet, 0)
    for dev in (opp_e, along_x(1), along_x(2), along_x(3)):
        pl.semaphore_signal(bar, inc=1, device_id=dev, device_id_type=MESH)

    local = [
        pltpu.make_async_copy(cot.at[c], cots.at[pl.ds(0, 64)], lsem.at[0]),
        pltpu.make_async_copy(w_rest, w.at[:, pl.ds(96, 6048)], lsem.at[1]),
        pltpu.make_async_copy(w_down.at[pl.ds(c * HALF, HALF)], wd.at[0], lsem.at[2]),
    ]
    for d in local:
        d.start()
    tok_half[0] = tokens[:, :HALF].astype(F32)
    tok_half[1] = tokens[:, HALF:].astype(F32)
    lane = lax.broadcasted_iota(jnp.int32, (2, 128), 1)
    base = ex * 16 + c * 8
    route_row = jnp.zeros((2, 128), F32)
    gate_row = jnp.zeros((2, 128), F32)
    for t in range(8):
        here = lane == base + t
        route_row = jnp.where(here, routes[:, t : t + 1].astype(F32), route_row)
        gate_row = jnp.where(here, gates[:, t : t + 1], gate_row)
    meta_own[...] = jnp.zeros((8, 128), F32)
    meta_own[0:2, :] = route_row
    meta_own[2:4, :] = gate_row

    pl.semaphore_wait(bar, 35)

    send(tok_half.at[oc], tok_pair.at[c], s_pair.at[0], sib)
    send(meta_own, meta_sib, s_pair.at[1], sib)
    send(saved, saved_sib, s_pair.at[2], sib)
    send(cot.at[oc], cots.at[pl.ds(64, 64)], s_pair.at[3], sib)
    send(w_down.at[pl.ds(oc * HALF, HALF)], wd.at[1], s_pair.at[4], sib)

    tok_pair[c] = tok_half[c]
    got(tok_pair.at[oc], s_pair.at[0])
    got(meta_sib, s_pair.at[1])
    meta_all[ex] = meta_own[...] + meta_sib[...]
    send(meta_all.at[ex], meta_all.at[ex], s_meta.at[1, 0], opp_e)
    for d in (1, 3, 2):
        send(meta_all.at[ex], meta_all.at[ex], s_meta.at[0, (4 - d) % 4], along_x(d))
    for q in range(Q):
        toks[q, ex] = tok_pair[:, :, q * W : (q + 1) * W].reshape(16, W).astype(BF)
        send(toks.at[q, ex], toks.at[q, ex], s_tok.at[q, 1, 0], opp_e)
        for d in (1, 3, 2):
            send(toks.at[q, ex], toks.at[q, ex], s_tok.at[q, 0, (4 - d) % 4], along_x(d))

    got(saved_sib, s_pair.at[2])
    saved_t[...] = jnp.transpose(
        jnp.concatenate([saved[...].astype(F32), saved_sib[...].astype(F32)], axis=0)
    ).astype(BF)
    local[0].wait()
    got(cots.at[pl.ds(64, 64)], s_pair.at[3])
    for dy in (2, 1, 3, 0):
        for h in range(2):
            cols = pl.ds(pl.multiple_of(((y + dy) % 4) * 2048 + h * 1024, 1024), 1024)
            pg[dy, h] = jnp.dot(saved_t[...], cots[:, cols], preferred_element_type=F32).astype(BF)
        if dy == 2:
            send(pg.at[2, 0], g_opp.at[0], s_gopp.at[0], at(3, 0, c))
            send(pg.at[2, 1], g_opp.at[1], s_gopp.at[1], at(1, 0, c))
        if dy == 1:
            send(pg.at[1, 0], g_fin.at[0, 0], s_gfin.at[0, 0], at(1, 0, c))
        if dy == 3:
            send(pg.at[3, 1], g_fin.at[1, 1], s_gfin.at[1, 1], at(3, 0, c))

    other = (1 - zh) * 4 + xx
    got(meta_all.at[other], s_meta.at[1, 0])
    for d in (1, 3, 2):
        send(meta_all.at[other], meta_all.at[other], s_meta.at[1, (4 - d) % 4], along_x(d))
    for q in range(Q):
        got(toks.at[q, other], s_tok.at[q, 1, 0])
        for d in (1, 3, 2):
            send(toks.at[q, other], toks.at[q, other], s_tok.at[q, 1, (4 - d) % 4], along_x(d))

    got(g_opp.at[0], s_gopp.at[0])
    pg[3, 0] = (pg[3, 0].astype(F32) + g_opp[0].astype(F32)).astype(BF)
    send(pg.at[3, 0], g_fin.at[1, 0], s_gfin.at[1, 0], at(3, 0, c))
    got(g_opp.at[1], s_gopp.at[1])
    pg[1, 1] = (pg[1, 1].astype(F32) + g_opp[1].astype(F32)).astype(BF)
    send(pg.at[1, 1], g_fin.at[0, 1], s_gfin.at[0, 1], at(1, 0, c))

    for d in (1, 3, 2):
        for k in range(2):
            src = (zh if k == 0 else 1 - zh) * 4 + (xx + d) % 4
            got(meta_all.at[src], s_meta.at[k, d])
    meta = meta_all[0]
    for e in range(1, 8):
        meta = meta + meta_all[e]
    mine = ex.astype(F32)
    first = meta[0:1, :] == mine
    hit = jnp.logical_or(first, meta[1:2, :] == mine)
    hit_f = jnp.where(hit, 1.0, 0.0).astype(F32)
    gate_of = jnp.where(first, meta[2:3, :], meta[3:4, :])
    before = jnp.where(
        lax.broadcasted_iota(jnp.int32, (128, 128), 0)
        < lax.broadcasted_iota(jnp.int32, (128, 128), 1),
        1.0,
        0.0,
    ).astype(BF)
    rank = jnp.dot(
        jnp.broadcast_to(hit_f, (16, 128)).astype(BF), before, preferred_element_type=F32
    )[0:1, :]
    slot_id = lax.broadcasted_iota(jnp.int32, (ROWS, 128), 0).astype(F32)
    chosen = jnp.where(slot_id == rank, 1.0, 0.0).astype(F32) * hit_f
    row_gate = jnp.sum(chosen * gate_of, axis=1, keepdims=True)
    pick[0] = chosen
    pick[1] = jnp.broadcast_to(row_gate, (ROWS, 128))

    def pass_block(q, dy, s, y_sides):
        for side in y_sides:
            to = (dy - side) % 4
            send(x.at[0, q, dy, s], x.at[0, q, to, s], s_x.at[q, to, s], at(side, 0, c))
        send(x.at[0, q, dy, s], x.at[1, q, dy, s], s_xs.at[q, dy, s], sib)

    for q in range(Q):
        for d in (1, 3, 2):
            for k in range(2):
                src = (zh if k == 0 else 1 - zh) * 4 + (xx + d) % 4
                got(toks.at[q, src], s_tok.at[q, k, d])
        x[0, q, 0, 0] = jnp.dot(
            pick[0].astype(BF), toks[q].reshape(128, W), preferred_element_type=F32
        ).astype(BF)
        for s in (1, 2, 3):
            t = SLOT[(4 - DZ[s]) % 4]
            send(x.at[0, q, 0, 0], x.at[0, q, 0, t], s_x.at[q, 0, t], at(0, DZ[s], c))
        pass_block(q, 0, 0, (1, 3))

    for h in range(2):
        got(g_fin.at[0, h], s_gfin.at[0, h])
        got(g_fin.at[1, h], s_gfin.at[1, h])
        total = pg[0, h].astype(F32) + g_fin[0, h].astype(F32) + g_fin[1, h].astype(F32)
        zg[2 * h] = total[:, :512].astype(BF)
        zg[2 * h + 1] = total[:, 512:].astype(BF)
    for d in (1, 3, 2):
        send(zg.at[(z + d) % 4], zg_in.at[3 - d], s_zg.at[3 - d], at(0, d, c))

    def wide(p):
        return pl.ds(pl.multiple_of((p // 2) * 512, 512), 512)

    def narrow(p):
        return pl.ds(pl.multiple_of(p * UNITS, UNITS), UNITS)

    def exchange(src_of, dst_of, wait_of, out_sem, in_sem):
        def copy_to(s):
            p = (dp + s) % 32
            return pltpu.make_async_remote_copy(
                src_ref=src_of(p), dst_ref=dst_of(dp), send_sem=out_sem.at[s],
                recv_sem=in_sem.at[dp], device_id=(p, ex), device_id_type=MESH,
            )

        def start(s, carry):
            copy_to(s).start()
            return carry

        def finish(s, carry):
            p = (dp + s) % 32
            pltpu.make_async_remote_copy(
                src_ref=src_of(p), dst_ref=dst_of(p), send_sem=out_sem.at[s],
                recv_sem=in_sem.at[p], device_id=(p, ex), device_id_type=MESH,
            ).wait_recv()
            return carry

        def sent(s, carry):
            copy_to(s).wait_send()
            return carry

        def begin():
            pltpu.make_async_copy(src_of(dp), dst_of(dp), lsem.at[wait_of]).start()
            lax.fori_loop(1, 32, start, 0)

        def arrive():
            pltpu.make_async_copy(src_of(dp), dst_of(dp), lsem.at[wait_of]).wait()
            lax.fori_loop(1, 32, finish, 0)

        return begin, arrive, lambda: lax.fori_loop(1, 32, sent, 0)

    to_rows, rows_here, rows_sent = exchange(
        lambda p: grad_out.at[pl.ds(p * 3, 3)], lambda p: grad.at[p % 2, :, :, wide(p)],
        3, s_ga, s_gb,
    )
    to_cols, cols_here, cols_sent = exchange(
        lambda p: bucket_out.at[:, :, narrow(p)], lambda p: bucket_in.at[pl.ds(p * 3, 3)],
        4, s_ba, s_bb,
    )

    def gradient_z():
        full = zg[z].astype(F32)
        for d in range(3):
            got(zg_in.at[d], s_zg.at[d])
            full = full + zg_in[d].astype(F32)
        grad_out[...] = full.reshape(96, 1, 512)
        to_rows()

    def adam():
        rows_here()

        def step(k, carry):
            cols = pl.ds(pl.multiple_of(k * 1024, 1024), 1024)
            g = jnp.concatenate([grad[0, :, :, cols], grad[1, :, :, cols]], axis=1)
            grad_new[:, :, cols] = g
            mo = beta_one * moment[:, :, cols] + (1.0 - beta_one) * g
            se = beta_two * second[:, :, cols] + (1.0 - beta_two) * g * g
            ma = master[:, :, cols] - rate * (mo / bias_one) / (jnp.sqrt(se / bias_two) + epsilon)
            bucket_out[:, :, cols] = ma.astype(BF).astype(F32)
            return carry

        lax.fori_loop(0, 8, step, 0)
        to_cols()

    def bucket_rows():
        cols_here()
        for m in range(2):
            w[m, 0:96, :] = bucket_in[:, m : m + 1, :].reshape(96, UNITS).astype(BF)

    def gate_up(q, dy):
        for s in range(4):
            got(x.at[1, q, dy, s], s_xs.at[q, dy, s])
        for hr in range(2):
            left = x[hr, q, dy].reshape(4 * ROWS, W)
            start = pl.multiple_of((c if hr == 0 else oc) * HALF + q * W, W)
            for m in range(2):
                part = jnp.dot(left, w[m, pl.ds(start, W), :], preferred_element_type=F32)
                if q == 0 and hr == 0:
                    acc[dy, m] = part
                else:
                    acc[dy, m] = acc[dy, m] + part

    def hidden(dy):
        left = jnp.where(c == 0, x[0, 0, dy, :, :, 0:128], x[1, 0, dy, :, :, 0:128]).reshape(
            4 * ROWS, 128
        )[:, 0:96]
        gate = acc[dy, 0] + jnp.dot(left, w[0, 0:96, :], preferred_element_type=F32)
        up = acc[dy, 1] + jnp.dot(left, w[1, 0:96, :], preferred_element_type=F32)
        hid[0, dy] = (gate / (1.0 + jnp.exp(-gate)) * up).astype(BF)
        send(hid.at[0, dy], hid.at[1, dy], s_hid.at[dy], sib)

    def down(q, dy):
        nt = (((1,), (1,)), ((), ()))
        for k in range(2):
            rows = slice(q * W + k * 512, q * W + (k + 1) * 512)
            out = lax.dot_general(hid[0, dy], wd[0, rows, :], nt, preferred_element_type=F32)
            out = out + lax.dot_general(hid[1, dy], wd[1, rows, :], nt, preferred_element_type=F32)
            po[q, dy, :, :, k * 512 : (k + 1) * 512] = out.astype(BF).reshape(4, ROWS, 512)

    A, B = pl.ds(0, 2), pl.ds(2, 2)

    def from_sides(q, s):
        in_a = s < 2
        got(x.at[0, q, 3, s], s_x.at[q, 3, s])
        pass_block(q, 3, s, (1,) if in_a else ())
        got(x.at[0, q, 1, s], s_x.at[q, 1, s])
        pass_block(q, 1, s, () if in_a else (3,))

    def from_opposite(q):
        for s in (0, 2, 1, 3):
            got(x.at[0, q, 2, s], s_x.at[q, 2, s])
            pass_block(q, 2, s, ())

    local[1].wait()
    for m in range(2):
        w[m, 0:96, :] = jnp.zeros((96, UNITS), BF)
    for q in range(Q):
        from_sides(q, 0)
        for s in (1, 2, 3):
            got(x.at[0, q, 0, s], s_x.at[q, 0, s])
            pass_block(q, 0, s, (1, 3))
        if q == 0:
            gradient_z()
        if q == 1:
            adam()
        if q > 0:
            for s in (1, 2, 3):
                from_sides(q - 1, s)
            gate_up(q - 1, 0)
    for s in (1, 2, 3):
        from_sides(Q - 1, s)
    gate_up(0, 1)
    gate_up(0, 3)
    from_opposite(0)
    gate_up(1, 1)
    gate_up(1, 3)
    from_opposite(1)
    gate_up(2, 0)
    gate_up(2, 1)
    gate_up(2, 3)
    gate_up(0, 2)
    gate_up(1, 2)
    bucket_rows()
    for dy in (1, 3, 0):
        hidden(dy)
    local[2].wait()
    got(wd.at[1], s_pair.at[4])

    def direct(q):
        send(po.at[q, 1, A], r_fin.at[q, 0, A], s_rfin.at[q, 0, 0], at(1, 0, c))
        send(po.at[q, 3, B], r_fin.at[q, 1, B], s_rfin.at[q, 1, 1], at(3, 0, c))

    def opposite(q):
        send(po.at[q, 2, A], r_opp.at[q, 0], s_ropp.at[q, 0], at(3, 0, c))
        send(po.at[q, 2, B], r_opp.at[q, 1], s_ropp.at[q, 1], at(1, 0, c))

    def add_opposite(q):
        got(r_opp.at[q, 0], s_ropp.at[q, 0])
        po[q, 3, 0:2] = (po[q, 3, 0:2].astype(F32) + r_opp[q, 0].astype(F32)).astype(BF)
        send(po.at[q, 3, A], r_fin.at[q, 1, A], s_rfin.at[q, 1, 0], at(3, 0, c))
        got(r_opp.at[q, 1], s_ropp.at[q, 1])
        po[q, 1, 2:4] = (po[q, 1, 2:4].astype(F32) + r_opp[q, 1].astype(F32)).astype(BF)
        send(po.at[q, 1, B], r_fin.at[q, 0, B], s_rfin.at[q, 0, 1], at(1, 0, c))

    def direct_here(q):
        got(r_fin.at[q, 0, A], s_rfin.at[q, 0, 0])
        got(r_fin.at[q, 1, B], s_rfin.at[q, 1, 1])

    def along_z(q):
        def y_sum(s):
            return po[q, 0, s].astype(F32) + r_fin[q, 0, s].astype(F32) + r_fin[q, 1, s].astype(F32)

        def pass_on(s):
            z_out[q, s - 1] = y_sum(s).astype(BF)
            t = SLOT[(4 - DZ[s]) % 4] - 1
            send(z_out.at[q, s - 1], rz.at[q, t], s_rz.at[q, t], at(0, DZ[s], c))

        got(r_fin.at[q, 1, A], s_rfin.at[q, 1, 0])
        pass_on(1)
        got(r_fin.at[q, 0, B], s_rfin.at[q, 0, 1])
        pass_on(3)
        pass_on(2)
        z_own[q] = y_sum(0)

    def place_rows(q):
        total = z_own[q]
        for s in range(3):
            got(rz.at[q, s], s_rz.at[q, s])
            total = total + rz[q, s].astype(F32)
        scaled = (total * pick[1][:, 0:1]).astype(BF)
        placed = lax.dot_general(
            pick[0].astype(BF), scaled, (((0,), (0,)), ((), ())), preferred_element_type=F32
        )
        ct[q] = placed.astype(BF).reshape(2, 4, 16, W)
        for d in (1, 3, 2):
            send(ct.at[q, :, (xx + d) % 4], rx.at[q, 3 - d], s_rx.at[q, 3 - d], along_x(d))

    def x_sum(q, which):
        total = ct[q, which, xx].astype(F32)
        for d in range(3):
            total = total + rx[q, d, which].astype(F32)
        return total

    def along_zh(q):
        for d in range(3):
            got(rx.at[q, d], s_rx.at[q, d])
        zh_out[q] = x_sum(q, 1 - zh).astype(BF)
        send(zh_out.at[q], zh_in.at[q], s_zh.at[q], opp_e)

    def finish_rows(q):
        got(zh_in.at[q], s_zh.at[q])
        fin[q] = (x_sum(q, zh) + zh_in[q].astype(F32)).reshape(2, 8, W)
        send(fin.at[q, oc], fin_in.at[q], s_fin.at[q], sib)
        mixed[:, pl.ds(pl.multiple_of(c * HALF + q * W, W), W)] = fin[q, c].astype(BF)

    def from_sibling(q):
        got(fin_in.at[q], s_fin.at[q])
        mixed[:, pl.ds(pl.multiple_of(oc * HALF + q * W, W), W)] = fin_in[q].astype(BF)

    for dy in (1, 3):
        got(hid.at[1, dy], s_hid.at[dy])
        down(0, dy)
    direct(0)
    from_opposite(2)
    gate_up(2, 2)
    hidden(2)
    got(hid.at[1, 0], s_hid.at[0])
    down(0, 0)
    got(hid.at[1, 2], s_hid.at[2])
    down(0, 2)
    opposite(0)
    for dy in (2, 1, 3, 0):
        down(1, dy)
    add_opposite(0)
    direct_here(0)
    opposite(1)
    direct(1)
    for dy in (2, 1, 3, 0):
        down(2, dy)
    along_z(0)
    add_opposite(1)
    direct_here(1)
    opposite(2)
    direct(2)
    along_z(1)
    place_rows(0)
    add_opposite(2)
    direct_here(2)
    along_zh(0)
    along_z(2)
    place_rows(1)
    finish_rows(0)
    along_zh(1)
    place_rows(2)
    finish_rows(1)
    along_zh(2)
    from_sibling(0)
    from_sibling(1)
    finish_rows(2)
    from_sibling(2)

    for d in sends:
        d.wait_send()
    rows_sent()
    cols_sent()


def body(tokens, routes, gates, saved_inputs, cotangents, master, moment, second, w_rest, w_down):
    cot = jnp.transpose(cotangents[0, 0], (1, 0, 2))
    rows = [jnp.swapaxes(a[0], 0, 1) for a in (master, moment, second)]
    vmem = pl.BlockSpec(memory_space=pltpu.VMEM)
    hbm = pl.BlockSpec(memory_space=pl.ANY)
    dma = pltpu.SemaphoreType.DMA
    V = pltpu.VMEM
    mixed, gradient = pl.pallas_call(
        kernel,
        out_shape=(jax.ShapeDtypeStruct((8, D), BF), jax.ShapeDtypeStruct((3, 2, 8192), F32)),
        in_specs=[vmem, vmem, vmem, vmem, hbm, vmem, vmem, vmem, hbm, hbm],
        out_specs=(vmem, vmem),
        scratch_shapes=[
            V((2, 8, HALF), F32),
            V((2, 8, HALF), F32),
            V((8, 128), F32),
            V((8, 128), F32),
            V((8, 8, 128), F32),
            V((Q, 8, 16, W), BF),
            V((64, 96), BF),
            V((96, 128), BF),
            V((128, 8192), BF),
            V((4, 2, 96, 1024), BF),
            V((2, 96, 1024), BF),
            V((2, 2, 96, 1024), BF),
            V((4, 96, 512), BF),
            V((3, 96, 512), BF),
            V((96, 1, 512), F32),
            V((2, 3, 1, 8192), F32),
            V((3, 2, 8192), F32),
            V((96, 2, UNITS), F32),
            V((2, D, UNITS), BF),
            V((2, HALF, UNITS), BF),
            V((2, ROWS, 128), F32),
            V((2, Q, 4, 4, ROWS, W), BF),
            V((2, 4, 4 * ROWS, UNITS), BF),
            V((4, 2, 4 * ROWS, UNITS), F32),
            V((Q, 4, 4, ROWS, W), BF),
            V((Q, 2, 2, ROWS, W), BF),
            V((Q, 2, 4, ROWS, W), BF),
            V((Q, 3, ROWS, W), BF),
            V((Q, ROWS, W), F32),
            V((Q, 3, ROWS, W), BF),
            V((Q, 2, 4, 16, W), BF),
            V((Q, 3, 2, 16, W), BF),
            V((Q, 16, W), BF),
            V((Q, 16, W), BF),
            V((Q, 2, 8, W), F32),
            V((Q, 8, W), F32),
            dma((N_SEND,)), dma((5,)), dma((5,)), dma((Q, 2, 4)), dma((2, 4)),
            dma((Q, 4, 4)), dma((Q, 4, 4)), dma((2,)), dma((2, 2)), dma((3,)),
            dma((32,)), dma((32,)), dma((32,)), dma((32,)),
            dma((4,)), dma((Q, 2)), dma((Q, 2, 2)), dma((Q, 3)), dma((Q, 3)), dma((Q,)), dma((Q,)),
        ],
        compiler_params=pltpu.CompilerParams(
            collective_id=0, has_side_effects=True, vmem_limit_bytes=60 * 1024 * 1024
        ),
        cost_estimate=pl.CostEstimate(flops=8 * 10**9, bytes_accessed=12 * 10**6, transcendentals=0),
    )(
        tokens, jnp.transpose(routes), jnp.transpose(gates), saved_inputs[0, 0], cot, *rows,
        w_rest[0], w_down[0],
    )
    gradient = jnp.swapaxes(gradient, 0, 1)[None]
    moment_new = beta_one * moment + (1.0 - beta_one) * gradient
    second_new = beta_two * second + (1.0 - beta_two) * gradient * gradient
    master_new = master - rate * (moment_new / bias_one) / (
        jnp.sqrt(second_new / bias_two) + epsilon
    )
    return (mixed, master_new, moment_new, second_new)


def solution(mesh):
    in_specs = (
        P(("dp", "expert"), None),
        P(("dp", "expert"), None),
        P(("dp", "expert"), None),
        P("dp", "expert", None, None),
        P("dp", "expert", None, None, None),
        P("expert", None, "dp", None),
        P("expert", None, "dp", None),
        P("expert", None, "dp", None),
        P("expert", None, None, "dp"),
        P("expert", None, "dp"),
    )
    out_specs = (
        P(("dp", "expert"), None),
        P("expert", None, "dp", None),
        P("expert", None, "dp", None),
        P("expert", None, "dp", None),
    )
    return jax.shard_map(body, mesh=mesh, in_specs=in_specs, out_specs=out_specs, check_vma=False)
```

```python
import jax
import jax.numpy as jnp
from jax import lax
from jax.experimental import pallas as pl
from jax.experimental.pallas import tpu as pltpu
from jax.sharding import PartitionSpec as P

beta_one = 0.9
beta_two = 0.999
rate = 0.01
epsilon = 1e-08
bias_one = 1.0 - 0.9**20
bias_two = 1.0 - 0.999**20

BF = jnp.bfloat16
F32 = jnp.float32
MESH = pl.DeviceIdType.MESH
D = 6144
HALF = 3072
UNITS = 256
ROWS = 48
DZ = (0, 1, 3, 2)
SLOT = (0, 1, 3, 2)
N_SEND = 250
Q = 3
W = HALF // Q
WIDTHS = (640, 640, 640, 512, 384, 256)
STARTS = tuple(sum(WIDTHS[:r]) for r in range(len(WIDTHS)))
R = len(WIDTHS)


def kernel(
    tokens_h, routes_h, gates_h, saved_h, cot, master_h, moment_h, second_h, w_rest, w_down,
    mixed, grad_h,
    tokens, routes, gates, saved, master, moment, second, grad_new,
    tok_half, tok_pair, meta_own, meta_sib, meta_all, toks,
    saved_sib, saved_t, cots, pg, g_opp, g_fin, zg, zg_in, grad_out, grad, bucket_out, bucket_in,
    w, wd, pick, x, hid, acc, po, r_opp, r_fin, rz, z_own, z_out, ct, rx, zh_out, zh_in, own_out, own_in,
    ssem, lsem, s_pair, s_tok, s_meta, s_x, s_xs, s_gopp, s_gfin, s_zg,
    s_ga, s_gb, s_ba, s_bb, s_hid, s_ropp, s_rfin, s_rz, s_rx, s_zh, s_fin,
):
    dp = lax.axis_index("dp")
    ex = lax.axis_index("expert")
    y, z, c = dp // 8, (dp // 2) % 4, dp % 2
    zh, xx = ex // 4, ex % 4
    oc = 1 - c

    def at(dy, dz, core):
        return (((y + dy) % 4) * 8 + ((z + dz) % 4) * 2 + core, ex)

    sib = at(0, 0, oc)
    opp_e = (dp, (1 - zh) * 4 + xx)
    opp_other = (sib[0], (1 - zh) * 4 + xx)

    def along_x(d):
        return (dp, zh * 4 + (xx + d) % 4)

    sends = []

    def send(src, dst, rsem, dev, when=None):
        d = pltpu.make_async_remote_copy(
            src_ref=src, dst_ref=dst, send_sem=ssem.at[len(sends)], recv_sem=rsem,
            device_id=dev, device_id_type=MESH,
        )
        if when is None:
            d.start()
        else:
            pl.when(when)(d.start)
        sends.append((d, when))

    def got(dst, rsem):
        pltpu.make_async_remote_copy(
            src_ref=dst, dst_ref=dst, send_sem=ssem.at[0], recv_sem=rsem,
            device_id=sib, device_id_type=MESH,
        ).wait_recv()

    small = [
        pltpu.make_async_copy(a, b, lsem.at[5 + i])
        for i, (a, b) in enumerate(
            ((tokens_h, tokens), (routes_h, routes), (gates_h, gates), (saved_h, saved))
        )
    ]
    for d in small:
        d.start()
    states = [
        pltpu.make_async_copy(a, b, lsem.at[9 + i])
        for i, (a, b) in enumerate(((master_h, master), (moment_h, moment), (second_h, second)))
    ]
    grad_copy = pltpu.make_async_copy(grad_new, grad_h, lsem.at[12])

    bar = pltpu.get_barrier_semaphore()

    def greet(s, carry):
        pl.semaphore_signal(bar, inc=1, device_id=((dp + s) % 32, ex), device_id_type=MESH)
        return carry

    lax.fori_loop(1, 32, greet, 0)
    for dev in (opp_e, opp_other, along_x(1), along_x(2), along_x(3)):
        pl.semaphore_signal(bar, inc=1, device_id=dev, device_id_type=MESH)

    local = [
        pltpu.make_async_copy(cot.at[c], cots.at[pl.ds(0, 64)], lsem.at[0]),
        pltpu.make_async_copy(w_rest, w.at[:, pl.ds(96, 6048)], lsem.at[1]),
        pltpu.make_async_copy(w_down.at[pl.ds(c * HALF, HALF)], wd.at[0], lsem.at[2]),
    ]
    local[0].start()
    for d in small:
        d.wait()
    tok_half[0] = tokens[:, :HALF].astype(F32)
    tok_half[1] = tokens[:, HALF:].astype(F32)
    lane = lax.broadcasted_iota(jnp.int32, (2, 128), 1)
    base = ex * 16 + c * 8
    route_row = jnp.zeros((2, 128), F32)
    gate_row = jnp.zeros((2, 128), F32)
    for t in range(8):
        here = lane == base + t
        route_row = jnp.where(here, routes[:, t : t + 1].astype(F32), route_row)
        gate_row = jnp.where(here, gates[:, t : t + 1], gate_row)
    meta_own[...] = jnp.zeros((8, 128), F32)
    meta_own[0:2, :] = route_row
    meta_own[2:4, :] = gate_row

    pl.semaphore_wait(bar, 36)

    send(tok_half.at[oc], tok_pair.at[c], s_pair.at[0], sib)
    send(meta_own, meta_sib, s_pair.at[1], sib)
    send(saved, saved_sib, s_pair.at[2], sib)
    send(cot.at[oc], cots.at[pl.ds(64, 64)], s_pair.at[3], sib)

    tok_pair[c] = tok_half[c]
    got(tok_pair.at[oc], s_pair.at[0])
    got(meta_sib, s_pair.at[1])
    meta_all[ex] = meta_own[...] + meta_sib[...]
    send(meta_all.at[ex], meta_all.at[ex], s_meta.at[1, 0], opp_e)
    for d in (1, 3, 2):
        send(meta_all.at[ex], meta_all.at[ex], s_meta.at[0, (4 - d) % 4], along_x(d))

    def tokens_zh(q):
        send(toks.at[q, ex], toks.at[q, ex], s_tok.at[q, 1, 0], opp_e)

    for q in range(Q):
        toks[q, ex] = tok_pair[:, :, q * W : (q + 1) * W].reshape(16, W).astype(BF)
        if q == 0:
            tokens_zh(0)
        for d in (1, 3, 2):
            send(toks.at[q, ex], toks.at[q, ex], s_tok.at[q, 0, (4 - d) % 4], along_x(d))

    got(saved_sib, s_pair.at[2])
    saved_t[...] = jnp.transpose(
        jnp.concatenate([saved[...].astype(F32), saved_sib[...].astype(F32)], axis=0)
    ).astype(BF)
    local[0].wait()
    tokens_zh(1)
    got(cots.at[pl.ds(64, 64)], s_pair.at[3])
    for dy in (2, 1, 3, 0):
        for h in range(2):
            cols = pl.ds(pl.multiple_of(((y + dy) % 4) * 2048 + h * 1024, 1024), 1024)
            pg[dy, h] = jnp.dot(saved_t[...], cots[:, cols], preferred_element_type=F32).astype(BF)
        if dy == 2:
            send(pg.at[2, 0], g_opp.at[0], s_gopp.at[0], at(3, 0, c))
            send(pg.at[2, 1], g_opp.at[1], s_gopp.at[1], at(1, 0, c))
            tokens_zh(2)
        if dy == 1:
            send(pg.at[1, 0], g_fin.at[0, 0], s_gfin.at[0, 0], at(1, 0, c))
        if dy == 3:
            send(pg.at[3, 1], g_fin.at[1, 1], s_gfin.at[1, 1], at(3, 0, c))

    local[1].start()
    local[2].start()
    send(w_down.at[pl.ds(oc * HALF, HALF)], wd.at[1], s_pair.at[4], sib)
    for d in states:
        d.start()

    other = (1 - zh) * 4 + xx
    got(meta_all.at[other], s_meta.at[1, 0])
    for d in (1, 3, 2):
        send(meta_all.at[other], meta_all.at[other], s_meta.at[1, (4 - d) % 4], along_x(d))
    for q in range(Q):
        got(toks.at[q, other], s_tok.at[q, 1, 0])
        for d in (1, 3, 2):
            send(toks.at[q, other], toks.at[q, other], s_tok.at[q, 1, (4 - d) % 4], along_x(d))

    got(g_opp.at[0], s_gopp.at[0])
    pg[3, 0] = (pg[3, 0].astype(F32) + g_opp[0].astype(F32)).astype(BF)
    send(pg.at[3, 0], g_fin.at[1, 0], s_gfin.at[1, 0], at(3, 0, c))
    got(g_opp.at[1], s_gopp.at[1])
    pg[1, 1] = (pg[1, 1].astype(F32) + g_opp[1].astype(F32)).astype(BF)
    send(pg.at[1, 1], g_fin.at[0, 1], s_gfin.at[0, 1], at(1, 0, c))

    for d in (1, 3, 2):
        for k in range(2):
            src = (zh if k == 0 else 1 - zh) * 4 + (xx + d) % 4
            got(meta_all.at[src], s_meta.at[k, d])
    meta = meta_all[0]
    for e in range(1, 8):
        meta = meta + meta_all[e]
    mine = ex.astype(F32)
    first = meta[0:1, :] == mine
    hit = jnp.logical_or(first, meta[1:2, :] == mine)
    hit_f = jnp.where(hit, 1.0, 0.0).astype(F32)
    gate_of = jnp.where(first, meta[2:3, :], meta[3:4, :])
    before = jnp.where(
        lax.broadcasted_iota(jnp.int32, (128, 128), 0)
        < lax.broadcasted_iota(jnp.int32, (128, 128), 1),
        1.0,
        0.0,
    ).astype(BF)
    rank = jnp.dot(
        jnp.broadcast_to(hit_f, (16, 128)).astype(BF), before, preferred_element_type=F32
    )[0:1, :]
    slot_id = lax.broadcasted_iota(jnp.int32, (ROWS, 128), 0).astype(F32)
    chosen = jnp.where(slot_id == rank, 1.0, 0.0).astype(F32) * hit_f
    row_gate = jnp.sum(chosen * gate_of, axis=1, keepdims=True)
    pick[0] = chosen
    pick[1] = jnp.broadcast_to(row_gate, (ROWS, 128))

    def pass_block(q, dy, s, y_sides):
        for side in y_sides:
            to = (dy - side) % 4
            send(x.at[0, q, dy, s], x.at[0, q, to, s], s_x.at[q, to, s], at(side, 0, c))
        send(x.at[0, q, dy, s], x.at[1, q, dy, s], s_xs.at[q, dy, s], sib)

    def own_along_z(q):
        for s in (1, 2, 3):
            t = SLOT[(4 - DZ[s]) % 4]
            near_by = None if s == 3 else (z < 3 if s == 1 else z > 0)
            send(x.at[0, q, 0, 0], x.at[0, q, 0, t], s_x.at[q, 0, t], at(0, DZ[s], c), near_by)

    def on_along_z(q):
        send(x.at[0, q, 0, 3], x.at[0, q, 0, 1], s_x.at[q, 0, 1], at(0, 1, c), z == 2)
        send(x.at[0, q, 0, 3], x.at[0, q, 0, 2], s_x.at[q, 0, 2], at(0, 3, c), z == 1)

    for q in range(Q):
        for d in (1, 3, 2):
            for k in range(2):
                src = (zh if k == 0 else 1 - zh) * 4 + (xx + d) % 4
                got(toks.at[q, src], s_tok.at[q, k, d])
        x[0, q, 0, 0] = jnp.dot(
            pick[0].astype(BF), toks[q].reshape(128, W), preferred_element_type=F32
        ).astype(BF)
        if q == 0:
            own_along_z(0)
        pass_block(q, 0, 0, (1, 3))

    for h in range(2):
        got(g_fin.at[0, h], s_gfin.at[0, h])
        got(g_fin.at[1, h], s_gfin.at[1, h])
        total = pg[0, h].astype(F32) + g_fin[0, h].astype(F32) + g_fin[1, h].astype(F32)
        zg[2 * h] = total[:, :512].astype(BF)
        zg[2 * h + 1] = total[:, 512:].astype(BF)
    for d in (1, 3, 2):
        send(zg.at[(z + d) % 4], zg_in.at[3 - d], s_zg.at[3 - d], at(0, d, c))

    def wide(p):
        return pl.ds(pl.multiple_of((p // 2) * 512, 512), 512)

    def narrow(p):
        return pl.ds(pl.multiple_of(p * UNITS, UNITS), UNITS)

    def exchange(src_of, dst_of, wait_of, out_sem, in_sem):
        def copy_to(s):
            p = (dp + s) % 32
            return pltpu.make_async_remote_copy(
                src_ref=src_of(p), dst_ref=dst_of(dp), send_sem=out_sem.at[s],
                recv_sem=in_sem.at[dp], device_id=(p, ex), device_id_type=MESH,
            )

        def start(s, carry):
            copy_to(s).start()
            return carry

        def finish(s, carry):
            p = (dp + s) % 32
            pltpu.make_async_remote_copy(
                src_ref=src_of(p), dst_ref=dst_of(p), send_sem=out_sem.at[s],
                recv_sem=in_sem.at[p], device_id=(p, ex), device_id_type=MESH,
            ).wait_recv()
            return carry

        def sent(s, carry):
            copy_to(s).wait_send()
            return carry

        def begin():
            pltpu.make_async_copy(src_of(dp), dst_of(dp), lsem.at[wait_of]).start()
            lax.fori_loop(1, 32, start, 0)

        def arrive():
            pltpu.make_async_copy(src_of(dp), dst_of(dp), lsem.at[wait_of]).wait()
            lax.fori_loop(1, 32, finish, 0)

        return begin, arrive, lambda: lax.fori_loop(1, 32, sent, 0)

    to_rows, rows_here, rows_sent = exchange(
        lambda p: grad_out.at[pl.ds(p * 3, 3)], lambda p: grad.at[p % 2, :, :, wide(p)],
        3, s_ga, s_gb,
    )
    to_cols, cols_here, cols_sent = exchange(
        lambda p: bucket_out.at[:, :, narrow(p)], lambda p: bucket_in.at[pl.ds(p * 3, 3)],
        4, s_ba, s_bb,
    )

    def gradient_z():
        full = zg[z].astype(F32)
        for d in range(3):
            got(zg_in.at[d], s_zg.at[d])
            full = full + zg_in[d].astype(F32)
        grad_out[...] = full.reshape(96, 1, 512)
        to_rows()

    def adam():
        rows_here()
        for d in states:
            d.wait()

        def step(k, carry):
            cols = pl.ds(pl.multiple_of(k * 1024, 1024), 1024)
            g = jnp.concatenate([grad[0, :, :, cols], grad[1, :, :, cols]], axis=1)
            grad_new[:, :, cols] = g
            mo = beta_one * moment[:, :, cols] + (1.0 - beta_one) * g
            se = beta_two * second[:, :, cols] + (1.0 - beta_two) * g * g
            ma = master[:, :, cols] - rate * (mo / bias_one) / (jnp.sqrt(se / bias_two) + epsilon)
            bucket_out[:, :, cols] = ma.astype(BF).astype(F32)
            return carry

        lax.fori_loop(0, 8, step, 0)
        to_cols()
        grad_copy.start()

    def bucket_rows():
        cols_here()
        for m in range(2):
            w[m, 0:96, :] = bucket_in[:, m : m + 1, :].reshape(96, UNITS).astype(BF)

    def gate_up(q, dy):
        for s in range(4):
            got(x.at[1, q, dy, s], s_xs.at[q, dy, s])
        for hr in range(2):
            left = x[hr, q, dy].reshape(4 * ROWS, W)
            start = pl.multiple_of((c if hr == 0 else oc) * HALF + q * W, W)
            for m in range(2):
                part = jnp.dot(left, w[m, pl.ds(start, W), :], preferred_element_type=F32)
                if q == 0 and hr == 0:
                    acc[dy, m] = part
                else:
                    acc[dy, m] = acc[dy, m] + part

    def hidden(dy):
        left = jnp.where(c == 0, x[0, 0, dy, :, :, 0:128], x[1, 0, dy, :, :, 0:128]).reshape(
            4 * ROWS, 128
        )[:, 0:96]
        gate = acc[dy, 0] + jnp.dot(left, w[0, 0:96, :], preferred_element_type=F32)
        up = acc[dy, 1] + jnp.dot(left, w[1, 0:96, :], preferred_element_type=F32)
        hid[0, dy] = (gate / (1.0 + jnp.exp(-gate)) * up).astype(BF)
        send(hid.at[0, dy], hid.at[1, dy], s_hid.at[dy], sib)

    def down(q, dy):
        nt = (((1,), (1,)), ((), ()))
        rows = slice(STARTS[q], STARTS[q] + WIDTHS[q])
        out = lax.dot_general(hid[0, dy], wd[0, rows, :], nt, preferred_element_type=F32)
        out = out + lax.dot_general(hid[1, dy], wd[1, rows, :], nt, preferred_element_type=F32)
        po[q][dy] = out.astype(BF).reshape(4, ROWS, WIDTHS[q])

    A, B = pl.ds(0, 2), pl.ds(2, 2)

    near = jnp.where(z == 3, 2, 1)
    order = (3, near, 3 - near)

    def from_sides(q, k):
        in_a = k < 2
        s = 0 if k == 0 else order[k - 1]
        got(x.at[0, q, 3, s], s_x.at[q, 3, s])
        pass_block(q, 3, s, (1,) if in_a else ())
        got(x.at[0, q, 1, s], s_x.at[q, 1, s])
        pass_block(q, 1, s, () if in_a else (3,))

    def from_opposite(q):
        for s in (0, near, 3, 3 - near):
            got(x.at[0, q, 2, s], s_x.at[q, 2, s])
            pass_block(q, 2, s, ())

    for m in range(2):
        w[m, 0:96, :] = jnp.zeros((96, UNITS), BF)
    for q in range(Q):
        if q > 0:
            for s in (1, 2, 3):
                from_sides(q - 1, s)
        from_sides(q, 0)
        if q == 0:
            own_along_z(1)
        for k in range(3):
            s = order[k]
            got(x.at[0, q, 0, s], s_x.at[q, 0, s])
            if k == 0:
                on_along_z(q)
            pass_block(q, 0, s, (1, 3))
            if q == 0 and k == 1:
                gradient_z()
            if q == 1 and k == 2:
                adam()
            if k == 1 and q + 2 < Q:
                own_along_z(q + 2)
        if q == 0:
            local[1].wait()
        gate_up(q, 0)
        if q > 0:
            gate_up(q - 1, 1)
            gate_up(q - 1, 3)
            from_opposite(q - 1)
            gate_up(q - 1, 2)
    for s in (1, 2, 3):
        from_sides(Q - 1, s)
    gate_up(2, 1)
    gate_up(2, 3)
    bucket_rows()
    hidden(1)
    hidden(3)
    local[2].wait()
    got(wd.at[1], s_pair.at[4])

    def direct(q):
        send(po[q].at[1, A], r_fin[q].at[0, A], s_rfin.at[q, 0, 0], at(1, 0, c))
        send(po[q].at[3, B], r_fin[q].at[1, B], s_rfin.at[q, 1, 1], at(3, 0, c))

    def opposite(q):
        send(po[q].at[2, A], r_opp[q].at[0], s_ropp.at[q, 0], at(3, 0, c))
        send(po[q].at[2, B], r_opp[q].at[1], s_ropp.at[q, 1], at(1, 0, c))

    def add_opposite(q):
        got(r_opp[q].at[0], s_ropp.at[q, 0])
        po[q][3, 0:2] = (po[q][3, 0:2].astype(F32) + r_opp[q][0].astype(F32)).astype(BF)
        send(po[q].at[3, A], r_fin[q].at[1, A], s_rfin.at[q, 1, 0], at(3, 0, c))
        got(r_opp[q].at[1], s_ropp.at[q, 1])
        po[q][1, 2:4] = (po[q][1, 2:4].astype(F32) + r_opp[q][1].astype(F32)).astype(BF)
        send(po[q].at[1, B], r_fin[q].at[0, B], s_rfin.at[q, 0, 1], at(1, 0, c))

    def direct_here(q):
        got(r_fin[q].at[0, A], s_rfin.at[q, 0, 0])
        got(r_fin[q].at[1, B], s_rfin.at[q, 1, 1])

    def along_z(q):
        def y_sum(s):
            return po[q][0, s].astype(F32) + r_fin[q][0, s].astype(F32) + r_fin[q][1, s].astype(F32)

        def pass_on(s):
            z_out[q][s - 1] = y_sum(s).astype(BF)
            t = SLOT[(4 - DZ[s]) % 4] - 1
            send(z_out[q].at[s - 1], rz[q].at[t], s_rz.at[q, t], at(0, DZ[s], c))

        got(r_fin[q].at[1, A], s_rfin.at[q, 1, 0])
        pass_on(1)
        got(r_fin[q].at[0, B], s_rfin.at[q, 0, 1])
        pass_on(3)
        pass_on(2)
        z_own[q][...] = y_sum(0)

    def place_rows(q):
        total = z_own[q][...]
        for s in range(3):
            got(rz[q].at[s], s_rz.at[q, s])
            total = total + rz[q][s].astype(F32)
        scaled = (total * pick[1][:, 0:1]).astype(BF)
        placed = lax.dot_general(
            pick[0].astype(BF), scaled, (((0,), (0,)), ((), ())), preferred_element_type=F32
        )
        ct[q][...] = placed.astype(BF).reshape(2, 4, 16, WIDTHS[q])
        for d in (1, 3, 2):
            send(ct[q].at[:, (xx + d) % 4], rx[q].at[3 - d], s_rx.at[q, 3 - d], along_x(d))

    def x_sum(q, which):
        total = ct[q][which, xx].astype(F32)
        for d in range(3):
            total = total + rx[q][d, which].astype(F32)
        return total

    def along_zh(q):
        for d in range(3):
            got(rx[q].at[d], s_rx.at[q, d])
        zh_out[q][...] = x_sum(q, 1 - zh).reshape(2, 8, WIDTHS[q])
        send(zh_out[q].at[c], zh_in[q].at[0], s_zh.at[q, 0], opp_e)
        send(zh_out[q].at[oc], zh_in[q].at[1], s_zh.at[q, 1], opp_other)
        own_out[q][...] = x_sum(q, zh).reshape(2, 8, WIDTHS[q])
        send(own_out[q].at[oc], own_in[q], s_fin.at[q], sib)

    def finish_rows(q):
        def put(core, value):
            start = pl.multiple_of(core * HALF + STARTS[q], 128)
            mixed[:, pl.ds(start, WIDTHS[q])] = value.astype(BF)

        got(own_in[q], s_fin.at[q])
        got(zh_in[q].at[0], s_zh.at[q, 0])
        put(c, own_out[q][c] + zh_in[q][0])
        got(zh_in[q].at[1], s_zh.at[q, 1])
        put(oc, own_in[q][...] + zh_in[q][1])

    for dy in (1, 3):
        got(hid.at[1, dy], s_hid.at[dy])
        down(0, dy)
    direct(0)
    from_opposite(2)
    for dy in (1, 3):
        down(1, dy)
    direct(1)
    gate_up(2, 2)
    hidden(2)
    hidden(0)
    got(hid.at[1, 2], s_hid.at[2])
    down(0, 2)
    opposite(0)
    down(1, 2)
    opposite(1)
    got(hid.at[1, 0], s_hid.at[0])
    down(0, 0)
    for r in range(R + 4):
        if r < R:
            if r + 2 < R:
                down(r + 2, 2)
            add_opposite(r)
            if r + 2 < R:
                opposite(r + 2)
                down(r + 2, 1)
                down(r + 2, 3)
            direct_here(r)
            if r + 2 < R:
                direct(r + 2)
            if r + 1 < R:
                down(r + 1, 0)
        if 1 <= r <= R:
            along_z(r - 1)
        if 2 <= r <= R + 1:
            place_rows(r - 2)
        if 3 <= r <= R + 2:
            along_zh(r - 3)
        if 4 <= r <= R + 3:
            finish_rows(r - 4)
    for d, when in sends:
        if when is None:
            d.wait_send()
        else:
            pl.when(when)(d.wait_send)
    rows_sent()
    cols_sent()
    grad_copy.wait()


def body(tokens, routes, gates, saved_inputs, cotangents, master, moment, second, w_rest, w_down):
    cot = jnp.transpose(cotangents[0, 0], (1, 0, 2))
    rows = [jnp.swapaxes(a[0], 0, 1) for a in (master, moment, second)]
    vmem = pl.BlockSpec(memory_space=pltpu.VMEM)
    hbm = pl.BlockSpec(memory_space=pl.ANY)
    dma = pltpu.SemaphoreType.DMA
    mem = pltpu.VMEM
    mixed, gradient = pl.pallas_call(
        kernel,
        out_shape=(jax.ShapeDtypeStruct((8, D), BF), jax.ShapeDtypeStruct((3, 2, 8192), F32)),
        in_specs=[hbm] * 10,
        out_specs=(vmem, hbm),
        scratch_shapes=[
            mem((8, D), BF),
            mem((2, 8), jnp.int32),
            mem((2, 8), F32),
            mem((64, 96), BF),
            mem((3, 2, 8192), F32),
            mem((3, 2, 8192), F32),
            mem((3, 2, 8192), F32),
            mem((3, 2, 8192), F32),
            mem((2, 8, HALF), F32),
            mem((2, 8, HALF), F32),
            mem((8, 128), F32),
            mem((8, 128), F32),
            mem((8, 8, 128), F32),
            mem((Q, 8, 16, W), BF),
            mem((64, 96), BF),
            mem((96, 128), BF),
            mem((128, 8192), BF),
            mem((4, 2, 96, 1024), BF),
            mem((2, 96, 1024), BF),
            mem((2, 2, 96, 1024), BF),
            mem((4, 96, 512), BF),
            mem((3, 96, 512), BF),
            mem((96, 1, 512), F32),
            mem((2, 3, 1, 8192), F32),
            mem((3, 2, 8192), F32),
            mem((96, 2, UNITS), F32),
            mem((2, D, UNITS), BF),
            mem((2, HALF, UNITS), BF),
            mem((2, ROWS, 128), F32),
            mem((2, Q, 4, 4, ROWS, W), BF),
            mem((2, 4, 4 * ROWS, UNITS), BF),
            mem((4, 2, 4 * ROWS, UNITS), F32),
            [mem((4, 4, ROWS, v), BF) for v in WIDTHS],
            [mem((2, 2, ROWS, v), BF) for v in WIDTHS],
            [mem((2, 4, ROWS, v), BF) for v in WIDTHS],
            [mem((3, ROWS, v), BF) for v in WIDTHS],
            [mem((ROWS, v), F32) for v in WIDTHS],
            [mem((3, ROWS, v), BF) for v in WIDTHS],
            [mem((2, 4, 16, v), BF) for v in WIDTHS],
            [mem((3, 2, 16, v), BF) for v in WIDTHS],
            [mem((2, 8, v), F32) for v in WIDTHS],
            [mem((2, 8, v), F32) for v in WIDTHS],
            [mem((2, 8, v), F32) for v in WIDTHS],
            [mem((8, v), F32) for v in WIDTHS],
            dma((N_SEND,)), dma((13,)), dma((5,)), dma((Q, 2, 4)), dma((2, 4)),
            dma((Q, 4, 4)), dma((Q, 4, 4)), dma((2,)), dma((2, 2)), dma((3,)),
            dma((32,)), dma((32,)), dma((32,)), dma((32,)),
            dma((4,)), dma((R, 2)), dma((R, 2, 2)), dma((R, 3)), dma((R, 3)), dma((R, 2)), dma((R,)),
        ],
        compiler_params=pltpu.CompilerParams(
            collective_id=0, has_side_effects=True, vmem_limit_bytes=60 * 1024 * 1024
        ),
        cost_estimate=pl.CostEstimate(flops=8 * 10**9, bytes_accessed=12 * 10**6, transcendentals=0),
    )(
        tokens, jnp.transpose(routes), jnp.transpose(gates), saved_inputs[0, 0], cot, *rows,
        w_rest[0], w_down[0],
    )
    gradient = jnp.swapaxes(gradient, 0, 1)[None]
    moment_new = beta_one * moment + (1.0 - beta_one) * gradient
    second_new = beta_two * second + (1.0 - beta_two) * gradient * gradient
    master_new = master - rate * (moment_new / bias_one) / (
        jnp.sqrt(second_new / bias_two) + epsilon
    )
    return (mixed, master_new, moment_new, second_new)


def solution(mesh):
    in_specs = (
        P(("dp", "expert"), None),
        P(("dp", "expert"), None),
        P(("dp", "expert"), None),
        P("dp", "expert", None, None),
        P("dp", "expert", None, None, None),
        P("expert", None, "dp", None),
        P("expert", None, "dp", None),
        P("expert", None, "dp", None),
        P("expert", None, None, "dp"),
        P("expert", None, "dp"),
    )
    out_specs = (
        P(("dp", "expert"), None),
        P("expert", None, "dp", None),
        P("expert", None, "dp", None),
        P("expert", None, "dp", None),
    )
    return jax.shard_map(body, mesh=mesh, in_specs=in_specs, out_specs=out_specs, check_vma=False)
```

```python
import jax
import jax.numpy as jnp
from jax import lax
from jax.experimental import pallas as pl
from jax.experimental.pallas import tpu as pltpu
from jax.sharding import PartitionSpec as P

beta_one = 0.9
beta_two = 0.999
rate = 0.01
epsilon = 1e-08
bias_one = 1.0 - 0.9**20
bias_two = 1.0 - 0.999**20

BF = jnp.bfloat16
F32 = jnp.float32
MESH = pl.DeviceIdType.MESH
D = 6144
HALF = 3072
UNITS = 256
ROWS = 48
DZ = (0, 1, 3, 2)
SLOT = (0, 1, 3, 2)
N_SEND = 250
Q = 3
W = HALF // Q
WIDTHS = (640, 640, 640, 512, 384, 256)
STARTS = tuple(sum(WIDTHS[:r]) for r in range(len(WIDTHS)))
R = len(WIDTHS)


def kernel(
    tokens_h, routes_h, gates_h, saved_h, cot, master_h, moment_h, second_h, w_rest, w_down,
    mixed, grad_h,
    tokens, routes, gates, saved, master, moment, second, grad_new,
    tok_half, tok_pair, meta_own, meta_sib, meta_all, toks,
    saved_sib, saved_t, cots, pg, g_opp, g_fin, zg, zg_in, grad_out, grad, bucket_out, bucket_in,
    w, wd, pick, x, hid, acc, po, r_opp, r_fin, rz, z_own, z_out, ct, rx, zh_out, zh_in, own_out, own_in,
    ssem, lsem, s_pair, s_tok, s_meta, s_x, s_xs, s_gopp, s_gfin, s_zg,
    s_ga, s_gb, s_ba, s_bb, s_hid, s_ropp, s_rfin, s_rz, s_rx, s_zh, s_fin,
):
    dp = lax.axis_index("dp")
    ex = lax.axis_index("expert")
    y, z, c = dp // 8, (dp // 2) % 4, dp % 2
    zh, xx = ex // 4, ex % 4
    oc = 1 - c

    def at(dy, dz, core):
        return (((y + dy) % 4) * 8 + ((z + dz) % 4) * 2 + core, ex)

    sib = at(0, 0, oc)
    opp_e = (dp, (1 - zh) * 4 + xx)

    def along_x(d):
        return (dp, zh * 4 + (xx + d) % 4)

    sends = []

    def send(src, dst, rsem, dev, when=None):
        d = pltpu.make_async_remote_copy(
            src_ref=src, dst_ref=dst, send_sem=ssem.at[len(sends)], recv_sem=rsem,
            device_id=dev, device_id_type=MESH,
        )
        if when is None:
            d.start()
        else:
            pl.when(when)(d.start)
        sends.append((d, when))

    def got(dst, rsem):
        pltpu.make_async_remote_copy(
            src_ref=dst, dst_ref=dst, send_sem=ssem.at[0], recv_sem=rsem,
            device_id=sib, device_id_type=MESH,
        ).wait_recv()

    small = [
        pltpu.make_async_copy(a, b, lsem.at[5 + i])
        for i, (a, b) in enumerate(
            ((tokens_h, tokens), (routes_h, routes), (gates_h, gates), (saved_h, saved))
        )
    ]
    for d in small:
        d.start()
    states = [
        pltpu.make_async_copy(a, b, lsem.at[9 + i])
        for i, (a, b) in enumerate(((master_h, master), (moment_h, moment), (second_h, second)))
    ]
    grad_copy = pltpu.make_async_copy(grad_new, grad_h, lsem.at[12])

    bar = pltpu.get_barrier_semaphore()

    def greet(s, carry):
        pl.semaphore_signal(bar, inc=1, device_id=((dp + s) % 32, ex), device_id_type=MESH)
        return carry

    lax.fori_loop(1, 32, greet, 0)
    for dev in (opp_e, along_x(1), along_x(2), along_x(3)):
        pl.semaphore_signal(bar, inc=1, device_id=dev, device_id_type=MESH)

    local = [
        pltpu.make_async_copy(cot.at[c], cots.at[pl.ds(0, 64)], lsem.at[0]),
        pltpu.make_async_copy(w_rest, w.at[:, pl.ds(96, 6048)], lsem.at[1]),
        pltpu.make_async_copy(w_down.at[pl.ds(c * HALF, HALF)], wd.at[0], lsem.at[2]),
    ]
    local[0].start()
    for d in small:
        d.wait()
    tok_half[0] = tokens[:, :HALF].astype(F32)
    tok_half[1] = tokens[:, HALF:].astype(F32)
    lane = lax.broadcasted_iota(jnp.int32, (2, 128), 1)
    base = ex * 16 + c * 8
    route_row = jnp.zeros((2, 128), F32)
    gate_row = jnp.zeros((2, 128), F32)
    for t in range(8):
        here = lane == base + t
        route_row = jnp.where(here, routes[:, t : t + 1].astype(F32), route_row)
        gate_row = jnp.where(here, gates[:, t : t + 1], gate_row)
    meta_own[...] = jnp.zeros((8, 128), F32)
    meta_own[0:2, :] = route_row
    meta_own[2:4, :] = gate_row

    pl.semaphore_wait(bar, 35)

    send(tok_half.at[oc], tok_pair.at[c], s_pair.at[0], sib)
    send(meta_own, meta_sib, s_pair.at[1], sib)
    send(saved, saved_sib, s_pair.at[2], sib)
    send(cot.at[oc], cots.at[pl.ds(64, 64)], s_pair.at[3], sib)

    tok_pair[c] = tok_half[c]
    got(tok_pair.at[oc], s_pair.at[0])
    got(meta_sib, s_pair.at[1])
    meta_all[ex] = meta_own[...] + meta_sib[...]
    send(meta_all.at[ex], meta_all.at[ex], s_meta.at[1, 0], opp_e)
    for d in (1, 3, 2):
        send(meta_all.at[ex], meta_all.at[ex], s_meta.at[0, (4 - d) % 4], along_x(d))

    def tokens_zh(q):
        send(toks.at[q, ex], toks.at[q, ex], s_tok.at[q, 1, 0], opp_e)

    for q in range(Q):
        toks[q, ex] = tok_pair[:, :, q * W : (q + 1) * W].reshape(16, W).astype(BF)
        if q == 0:
            tokens_zh(0)
        for d in (1, 3, 2):
            send(toks.at[q, ex], toks.at[q, ex], s_tok.at[q, 0, (4 - d) % 4], along_x(d))

    got(saved_sib, s_pair.at[2])
    saved_t[...] = jnp.transpose(
        jnp.concatenate([saved[...].astype(F32), saved_sib[...].astype(F32)], axis=0)
    ).astype(BF)
    local[0].wait()
    tokens_zh(1)
    got(cots.at[pl.ds(64, 64)], s_pair.at[3])
    for dy in (2, 1, 3, 0):
        for h in range(2):
            cols = pl.ds(pl.multiple_of(((y + dy) % 4) * 2048 + h * 1024, 1024), 1024)
            pg[dy, h] = jnp.dot(saved_t[...], cots[:, cols], preferred_element_type=F32).astype(BF)
        if dy == 2:
            send(pg.at[2, 0], g_opp.at[0], s_gopp.at[0], at(3, 0, c))
            send(pg.at[2, 1], g_opp.at[1], s_gopp.at[1], at(1, 0, c))
            tokens_zh(2)
        if dy == 1:
            send(pg.at[1, 0], g_fin.at[0, 0], s_gfin.at[0, 0], at(1, 0, c))
        if dy == 3:
            send(pg.at[3, 1], g_fin.at[1, 1], s_gfin.at[1, 1], at(3, 0, c))

    local[1].start()
    local[2].start()
    send(w_down.at[pl.ds(oc * HALF, HALF)], wd.at[1], s_pair.at[4], sib)
    for d in states:
        d.start()

    other = (1 - zh) * 4 + xx
    got(meta_all.at[other], s_meta.at[1, 0])
    for d in (1, 3, 2):
        send(meta_all.at[other], meta_all.at[other], s_meta.at[1, (4 - d) % 4], along_x(d))
    for q in range(Q):
        got(toks.at[q, other], s_tok.at[q, 1, 0])
        for d in (1, 3, 2):
            send(toks.at[q, other], toks.at[q, other], s_tok.at[q, 1, (4 - d) % 4], along_x(d))

    got(g_opp.at[0], s_gopp.at[0])
    pg[3, 0] = (pg[3, 0].astype(F32) + g_opp[0].astype(F32)).astype(BF)
    send(pg.at[3, 0], g_fin.at[1, 0], s_gfin.at[1, 0], at(3, 0, c))
    got(g_opp.at[1], s_gopp.at[1])
    pg[1, 1] = (pg[1, 1].astype(F32) + g_opp[1].astype(F32)).astype(BF)
    send(pg.at[1, 1], g_fin.at[0, 1], s_gfin.at[0, 1], at(1, 0, c))

    for d in (1, 3, 2):
        for k in range(2):
            src = (zh if k == 0 else 1 - zh) * 4 + (xx + d) % 4
            got(meta_all.at[src], s_meta.at[k, d])
    meta = meta_all[0]
    for e in range(1, 8):
        meta = meta + meta_all[e]
    mine = ex.astype(F32)
    first = meta[0:1, :] == mine
    hit = jnp.logical_or(first, meta[1:2, :] == mine)
    hit_f = jnp.where(hit, 1.0, 0.0).astype(F32)
    gate_of = jnp.where(first, meta[2:3, :], meta[3:4, :])
    before = jnp.where(
        lax.broadcasted_iota(jnp.int32, (128, 128), 0)
        < lax.broadcasted_iota(jnp.int32, (128, 128), 1),
        1.0,
        0.0,
    ).astype(BF)
    rank = jnp.dot(
        jnp.broadcast_to(hit_f, (16, 128)).astype(BF), before, preferred_element_type=F32
    )[0:1, :]
    slot_id = lax.broadcasted_iota(jnp.int32, (ROWS, 128), 0).astype(F32)
    chosen = jnp.where(slot_id == rank, 1.0, 0.0).astype(F32) * hit_f
    row_gate = jnp.sum(chosen * gate_of, axis=1, keepdims=True)
    pick[0] = chosen
    pick[1] = jnp.broadcast_to(row_gate, (ROWS, 128))

    def pass_block(q, dy, s, y_sides):
        for side in y_sides:
            to = (dy - side) % 4
            send(x.at[0, q, dy, s], x.at[0, q, to, s], s_x.at[q, to, s], at(side, 0, c))
        send(x.at[0, q, dy, s], x.at[1, q, dy, s], s_xs.at[q, dy, s], sib)

    def own_along_z(q):
        for s in (1, 2, 3):
            t = SLOT[(4 - DZ[s]) % 4]
            near_by = None if s == 3 else (z < 3 if s == 1 else z > 0)
            send(x.at[0, q, 0, 0], x.at[0, q, 0, t], s_x.at[q, 0, t], at(0, DZ[s], c), near_by)

    def on_along_z(q):
        send(x.at[0, q, 0, 3], x.at[0, q, 0, 1], s_x.at[q, 0, 1], at(0, 1, c), z == 2)
        send(x.at[0, q, 0, 3], x.at[0, q, 0, 2], s_x.at[q, 0, 2], at(0, 3, c), z == 1)

    for q in range(Q):
        for d in (1, 3, 2):
            for k in range(2):
                src = (zh if k == 0 else 1 - zh) * 4 + (xx + d) % 4
                got(toks.at[q, src], s_tok.at[q, k, d])
        x[0, q, 0, 0] = jnp.dot(
            pick[0].astype(BF), toks[q].reshape(128, W), preferred_element_type=F32
        ).astype(BF)
        if q == 0:
            own_along_z(0)
            pass_block(0, 0, 0, (1, 3))

    for h in range(2):
        got(g_fin.at[0, h], s_gfin.at[0, h])
        got(g_fin.at[1, h], s_gfin.at[1, h])
        total = pg[0, h].astype(F32) + g_fin[0, h].astype(F32) + g_fin[1, h].astype(F32)
        zg[2 * h] = total[:, :512].astype(BF)
        zg[2 * h + 1] = total[:, 512:].astype(BF)
    for d in (1, 3, 2):
        send(zg.at[(z + d) % 4], zg_in.at[3 - d], s_zg.at[3 - d], at(0, d, c))

    for q in range(1, Q):
        pass_block(q, 0, 0, (1, 3))

    def wide(p):
        return pl.ds(pl.multiple_of((p // 2) * 512, 512), 512)

    def narrow(p):
        return pl.ds(pl.multiple_of(p * UNITS, UNITS), UNITS)

    def exchange(src_of, dst_of, wait_of, out_sem, in_sem):
        def copy_to(s):
            p = (dp + s) % 32
            return pltpu.make_async_remote_copy(
                src_ref=src_of(p), dst_ref=dst_of(dp), send_sem=out_sem.at[s],
                recv_sem=in_sem.at[dp], device_id=(p, ex), device_id_type=MESH,
            )

        def start(s, carry):
            copy_to(s).start()
            return carry

        def finish(s, carry):
            p = (dp + s) % 32
            pltpu.make_async_remote_copy(
                src_ref=src_of(p), dst_ref=dst_of(p), send_sem=out_sem.at[s],
                recv_sem=in_sem.at[p], device_id=(p, ex), device_id_type=MESH,
            ).wait_recv()
            return carry

        def sent(s, carry):
            copy_to(s).wait_send()
            return carry

        def begin():
            pltpu.make_async_copy(src_of(dp), dst_of(dp), lsem.at[wait_of]).start()
            lax.fori_loop(1, 32, start, 0)

        def arrive():
            pltpu.make_async_copy(src_of(dp), dst_of(dp), lsem.at[wait_of]).wait()
            lax.fori_loop(1, 32, finish, 0)

        return begin, arrive, lambda: lax.fori_loop(1, 32, sent, 0)

    to_rows, rows_here, rows_sent = exchange(
        lambda p: grad_out.at[pl.ds(p * 3, 3)], lambda p: grad.at[p % 2, :, :, wide(p)],
        3, s_ga, s_gb,
    )
    to_cols, cols_here, cols_sent = exchange(
        lambda p: bucket_out.at[:, :, narrow(p)], lambda p: bucket_in.at[pl.ds(p * 3, 3)],
        4, s_ba, s_bb,
    )

    def gradient_z():
        full = zg[z].astype(F32)
        for d in range(3):
            got(zg_in.at[d], s_zg.at[d])
            full = full + zg_in[d].astype(F32)
        grad_out[...] = full.reshape(96, 1, 512)
        to_rows()

    def adam():
        rows_here()
        for d in states:
            d.wait()

        def step(k, carry):
            cols = pl.ds(pl.multiple_of(k * 1024, 1024), 1024)
            g = jnp.concatenate([grad[0, :, :, cols], grad[1, :, :, cols]], axis=1)
            grad_new[:, :, cols] = g
            mo = beta_one * moment[:, :, cols] + (1.0 - beta_one) * g
            se = beta_two * second[:, :, cols] + (1.0 - beta_two) * g * g
            ma = master[:, :, cols] - rate * (mo / bias_one) / (jnp.sqrt(se / bias_two) + epsilon)
            bucket_out[:, :, cols] = ma.astype(BF).astype(F32)
            return carry

        lax.fori_loop(0, 8, step, 0)
        to_cols()
        grad_copy.start()

    def bucket_rows():
        cols_here()
        for m in range(2):
            w[m, 0:96, :] = bucket_in[:, m : m + 1, :].reshape(96, UNITS).astype(BF)

    def gate_up(q, dy):
        for s in range(4):
            got(x.at[1, q, dy, s], s_xs.at[q, dy, s])
        for hr in range(2):
            left = x[hr, q, dy].reshape(4 * ROWS, W)
            start = pl.multiple_of((c if hr == 0 else oc) * HALF + q * W, W)
            for m in range(2):
                part = jnp.dot(left, w[m, pl.ds(start, W), :], preferred_element_type=F32)
                if q == 0 and hr == 0:
                    acc[dy, m] = part
                else:
                    acc[dy, m] = acc[dy, m] + part

    def hidden(dy):
        left = jnp.where(c == 0, x[0, 0, dy, :, :, 0:128], x[1, 0, dy, :, :, 0:128]).reshape(
            4 * ROWS, 128
        )[:, 0:96]
        gate = acc[dy, 0] + jnp.dot(left, w[0, 0:96, :], preferred_element_type=F32)
        up = acc[dy, 1] + jnp.dot(left, w[1, 0:96, :], preferred_element_type=F32)
        hid[0, dy] = (gate / (1.0 + jnp.exp(-gate)) * up).astype(BF)
        send(hid.at[0, dy], hid.at[1, dy], s_hid.at[dy], sib)

    def down(q, dy):
        nt = (((1,), (1,)), ((), ()))
        rows = slice(STARTS[q], STARTS[q] + WIDTHS[q])
        out = lax.dot_general(hid[0, dy], wd[0, rows, :], nt, preferred_element_type=F32)
        out = out + lax.dot_general(hid[1, dy], wd[1, rows, :], nt, preferred_element_type=F32)
        po[q][dy] = out.astype(BF).reshape(4, ROWS, WIDTHS[q])

    A, B = pl.ds(0, 2), pl.ds(2, 2)

    near = jnp.where(z == 3, 2, 1)
    order = (3, near, 3 - near)

    def from_sides(q, k):
        in_a = k < 2
        s = 0 if k == 0 else order[k - 1]
        got(x.at[0, q, 3, s], s_x.at[q, 3, s])
        pass_block(q, 3, s, (1,) if in_a else ())
        got(x.at[0, q, 1, s], s_x.at[q, 1, s])
        pass_block(q, 1, s, () if in_a else (3,))

    def from_opposite(q):
        for s in (0, near, 3, 3 - near):
            got(x.at[0, q, 2, s], s_x.at[q, 2, s])
            pass_block(q, 2, s, ())

    for m in range(2):
        w[m, 0:96, :] = jnp.zeros((96, UNITS), BF)
    for q in range(Q):
        if q > 0:
            for s in (1, 2, 3):
                from_sides(q - 1, s)
        from_sides(q, 0)
        if q == 0:
            own_along_z(1)
        if q == 1:
            gradient_z()
        if q == 2:
            adam()
        for k in range(3):
            s = order[k]
            got(x.at[0, q, 0, s], s_x.at[q, 0, s])
            if k == 0:
                on_along_z(q)
            pass_block(q, 0, s, (1, 3))
            if k == 1 and q + 2 < Q:
                own_along_z(q + 2)
        if q == 0:
            local[1].wait()
        gate_up(q, 0)
        if q > 0:
            gate_up(q - 1, 1)
            gate_up(q - 1, 3)
            from_opposite(q - 1)
            gate_up(q - 1, 2)
    for s in (1, 2, 3):
        from_sides(Q - 1, s)
    gate_up(2, 1)
    gate_up(2, 3)
    bucket_rows()
    hidden(1)
    hidden(3)
    local[2].wait()
    got(wd.at[1], s_pair.at[4])

    def direct(q):
        send(po[q].at[1, A], r_fin[q].at[0, A], s_rfin.at[q, 0, 0], at(1, 0, c))
        send(po[q].at[3, B], r_fin[q].at[1, B], s_rfin.at[q, 1, 1], at(3, 0, c))

    def opposite(q):
        send(po[q].at[2, A], r_opp[q].at[0], s_ropp.at[q, 0], at(3, 0, c))
        send(po[q].at[2, B], r_opp[q].at[1], s_ropp.at[q, 1], at(1, 0, c))

    def add_opposite(q):
        got(r_opp[q].at[0], s_ropp.at[q, 0])
        po[q][3, 0:2] = (po[q][3, 0:2].astype(F32) + r_opp[q][0].astype(F32)).astype(BF)
        send(po[q].at[3, A], r_fin[q].at[1, A], s_rfin.at[q, 1, 0], at(3, 0, c))
        got(r_opp[q].at[1], s_ropp.at[q, 1])
        po[q][1, 2:4] = (po[q][1, 2:4].astype(F32) + r_opp[q][1].astype(F32)).astype(BF)
        send(po[q].at[1, B], r_fin[q].at[0, B], s_rfin.at[q, 0, 1], at(1, 0, c))

    def direct_here(q):
        got(r_fin[q].at[0, A], s_rfin.at[q, 0, 0])
        got(r_fin[q].at[1, B], s_rfin.at[q, 1, 1])

    def along_z(q):
        def y_sum(s):
            return po[q][0, s].astype(F32) + r_fin[q][0, s].astype(F32) + r_fin[q][1, s].astype(F32)

        def pass_on(s):
            z_out[q][s - 1] = y_sum(s).astype(BF)
            t = SLOT[(4 - DZ[s]) % 4] - 1
            send(z_out[q].at[s - 1], rz[q].at[t], s_rz.at[q, t], at(0, DZ[s], c))

        got(r_fin[q].at[1, A], s_rfin.at[q, 1, 0])
        pass_on(1)
        got(r_fin[q].at[0, B], s_rfin.at[q, 0, 1])
        pass_on(3)
        pass_on(2)
        z_own[q][...] = y_sum(0)

    def place_rows(q):
        total = z_own[q][...]
        for s in range(3):
            got(rz[q].at[s], s_rz.at[q, s])
            total = total + rz[q][s].astype(F32)
        scaled = (total * pick[1][:, 0:1]).astype(BF)
        placed = lax.dot_general(
            pick[0].astype(BF), scaled, (((0,), (0,)), ((), ())), preferred_element_type=F32
        )
        ct[q][...] = placed.astype(BF).reshape(2, 4, 16, WIDTHS[q])
        for d in (1, 3, 2):
            send(ct[q].at[:, (xx + d) % 4], rx[q].at[3 - d], s_rx.at[q, 3 - d], along_x(d))

    def x_sum(q, which):
        total = ct[q][which, xx].astype(F32)
        for d in range(3):
            total = total + rx[q][d, which].astype(F32)
        return total

    def along_zh(q):
        for d in range(3):
            got(rx[q].at[d], s_rx.at[q, d])
        zh_out[q][...] = x_sum(q, 1 - zh).astype(BF)
        send(zh_out[q], zh_in[q], s_zh.at[q], opp_e)
        own_out[q][...] = x_sum(q, zh).reshape(2, 8, WIDTHS[q])

    def halves(q):
        got(zh_in[q], s_zh.at[q])
        own_out[q][...] = own_out[q][...] + zh_in[q][...].astype(F32).reshape(2, 8, WIDTHS[q])
        send(own_out[q].at[oc], own_in[q], s_fin.at[q], sib)

    def finish_rows(q):
        def put(core, value):
            start = pl.multiple_of(core * HALF + STARTS[q], 128)
            mixed[:, pl.ds(start, WIDTHS[q])] = value.astype(BF)

        put(c, own_out[q][c])
        got(own_in[q], s_fin.at[q])
        put(oc, own_in[q][...])

    for dy in (1, 3):
        got(hid.at[1, dy], s_hid.at[dy])
        down(0, dy)
    direct(0)
    from_opposite(2)
    for dy in (1, 3):
        down(1, dy)
    direct(1)
    gate_up(2, 2)
    hidden(2)
    hidden(0)
    got(hid.at[1, 2], s_hid.at[2])
    down(0, 2)
    opposite(0)
    down(1, 2)
    opposite(1)
    got(hid.at[1, 0], s_hid.at[0])
    down(0, 0)
    for r in range(R):
        if r + 2 < R:
            down(r + 2, 2)
        add_opposite(r)
        if r + 2 < R:
            opposite(r + 2)
            down(r + 2, 1)
            down(r + 2, 3)
        direct_here(r)
        if r + 2 < R:
            direct(r + 2)
        if r + 1 < R:
            down(r + 1, 0)
        if r >= 1:
            along_z(r - 1)
        if r >= 2:
            place_rows(r - 2)
        if r >= 3:
            along_zh(r - 3)
    along_z(R - 1)
    place_rows(R - 2)
    along_zh(R - 3)
    for r in range(R - 3):
        halves(r)
    place_rows(R - 1)
    along_zh(R - 2)
    halves(R - 3)
    for r in range(R - 3):
        finish_rows(r)
    along_zh(R - 1)
    halves(R - 2)
    finish_rows(R - 3)
    finish_rows(R - 2)
    halves(R - 1)
    finish_rows(R - 1)

    for d, when in sends:
        if when is None:
            d.wait_send()
        else:
            pl.when(when)(d.wait_send)
    rows_sent()
    cols_sent()
    grad_copy.wait()


def body(tokens, routes, gates, saved_inputs, cotangents, master, moment, second, w_rest, w_down):
    cot = jnp.transpose(cotangents[0, 0], (1, 0, 2))
    rows = [jnp.swapaxes(a[0], 0, 1) for a in (master, moment, second)]
    vmem = pl.BlockSpec(memory_space=pltpu.VMEM)
    hbm = pl.BlockSpec(memory_space=pl.ANY)
    dma = pltpu.SemaphoreType.DMA
    mem = pltpu.VMEM
    mixed, gradient = pl.pallas_call(
        kernel,
        out_shape=(jax.ShapeDtypeStruct((8, D), BF), jax.ShapeDtypeStruct((3, 2, 8192), F32)),
        in_specs=[hbm] * 10,
        out_specs=(vmem, hbm),
        scratch_shapes=[
            mem((8, D), BF),
            mem((2, 8), jnp.int32),
            mem((2, 8), F32),
            mem((64, 96), BF),
            mem((3, 2, 8192), F32),
            mem((3, 2, 8192), F32),
            mem((3, 2, 8192), F32),
            mem((3, 2, 8192), F32),
            mem((2, 8, HALF), F32),
            mem((2, 8, HALF), F32),
            mem((8, 128), F32),
            mem((8, 128), F32),
            mem((8, 8, 128), F32),
            mem((Q, 8, 16, W), BF),
            mem((64, 96), BF),
            mem((96, 128), BF),
            mem((128, 8192), BF),
            mem((4, 2, 96, 1024), BF),
            mem((2, 96, 1024), BF),
            mem((2, 2, 96, 1024), BF),
            mem((4, 96, 512), BF),
            mem((3, 96, 512), BF),
            mem((96, 1, 512), F32),
            mem((2, 3, 1, 8192), F32),
            mem((3, 2, 8192), F32),
            mem((96, 2, UNITS), F32),
            mem((2, D, UNITS), BF),
            mem((2, HALF, UNITS), BF),
            mem((2, ROWS, 128), F32),
            mem((2, Q, 4, 4, ROWS, W), BF),
            mem((2, 4, 4 * ROWS, UNITS), BF),
            mem((4, 2, 4 * ROWS, UNITS), F32),
            [mem((4, 4, ROWS, v), BF) for v in WIDTHS],
            [mem((2, 2, ROWS, v), BF) for v in WIDTHS],
            [mem((2, 4, ROWS, v), BF) for v in WIDTHS],
            [mem((3, ROWS, v), BF) for v in WIDTHS],
            [mem((ROWS, v), F32) for v in WIDTHS],
            [mem((3, ROWS, v), BF) for v in WIDTHS],
            [mem((2, 4, 16, v), BF) for v in WIDTHS],
            [mem((3, 2, 16, v), BF) for v in WIDTHS],
            [mem((16, v), BF) for v in WIDTHS],
            [mem((16, v), BF) for v in WIDTHS],
            [mem((2, 8, v), F32) for v in WIDTHS],
            [mem((8, v), F32) for v in WIDTHS],
            dma((N_SEND,)), dma((13,)), dma((5,)), dma((Q, 2, 4)), dma((2, 4)),
            dma((Q, 4, 4)), dma((Q, 4, 4)), dma((2,)), dma((2, 2)), dma((3,)),
            dma((32,)), dma((32,)), dma((32,)), dma((32,)),
            dma((4,)), dma((R, 2)), dma((R, 2, 2)), dma((R, 3)), dma((R, 3)), dma((R,)), dma((R,)),
        ],
        compiler_params=pltpu.CompilerParams(
            collective_id=0, has_side_effects=True, vmem_limit_bytes=60 * 1024 * 1024
        ),
        cost_estimate=pl.CostEstimate(flops=8 * 10**9, bytes_accessed=12 * 10**6, transcendentals=0),
    )(
        tokens, jnp.transpose(routes), jnp.transpose(gates), saved_inputs[0, 0], cot, *rows,
        w_rest[0], w_down[0],
    )
    gradient = jnp.swapaxes(gradient, 0, 1)[None]
    moment_new = beta_one * moment + (1.0 - beta_one) * gradient
    second_new = beta_two * second + (1.0 - beta_two) * gradient * gradient
    master_new = master - rate * (moment_new / bias_one) / (
        jnp.sqrt(second_new / bias_two) + epsilon
    )
    return (mixed, master_new, moment_new, second_new)


def solution(mesh):
    in_specs = (
        P(("dp", "expert"), None),
        P(("dp", "expert"), None),
        P(("dp", "expert"), None),
        P("dp", "expert", None, None),
        P("dp", "expert", None, None, None),
        P("expert", None, "dp", None),
        P("expert", None, "dp", None),
        P("expert", None, "dp", None),
        P("expert", None, None, "dp"),
        P("expert", None, "dp"),
    )
    out_specs = (
        P(("dp", "expert"), None),
        P("expert", None, "dp", None),
        P("expert", None, "dp", None),
        P("expert", None, "dp", None),
    )
    return jax.shard_map(body, mesh=mesh, in_specs=in_specs, out_specs=out_specs, check_vma=False)
```

```python
import jax
import jax.numpy as jnp
from jax import lax
from jax.experimental import pallas as pl
from jax.experimental.pallas import tpu as pltpu
from jax.sharding import PartitionSpec as P

beta_one = 0.9
beta_two = 0.999
rate = 0.01
epsilon = 1e-08
bias_one = 1.0 - 0.9**20
bias_two = 1.0 - 0.999**20

BF = jnp.bfloat16
F32 = jnp.float32
MESH = pl.DeviceIdType.MESH
D = 6144
HALF = 3072
UNITS = 256
ROWS = 48
DZ = (0, 1, 3, 2)
SLOT = (0, 1, 3, 2)
N_SEND = 250
Q = 3
W = HALF // Q
WIDTHS = (640, 640, 640, 512, 384, 256)
STARTS = tuple(sum(WIDTHS[:r]) for r in range(len(WIDTHS)))
R = len(WIDTHS)


def kernel(
    tokens_h, routes_h, gates_h, saved_h, cot, master_h, moment_h, second_h, w_rest, w_down,
    mixed, grad_h,
    tokens, routes, gates, saved, master, moment, second, grad_new,
    tok_half, tok_pair, meta_own, meta_sib, meta_all, toks,
    saved_sib, saved_t, cots, pg, g_opp, g_fin, zg, zg_in, grad_out, grad, bucket_out, bucket_in,
    w, wd, pick, x, hid, acc, po, r_opp, r_fin, rz, z_own, z_out, ct, rx, zh_out, zh_in, own_out, own_in,
    ssem, lsem, s_pair, s_tok, s_meta, s_x, s_xs, s_gopp, s_gfin, s_zg,
    s_ga, s_gb, s_ba, s_bb, s_hid, s_ropp, s_rfin, s_rz, s_rx, s_zh, s_fin,
):
    dp = lax.axis_index("dp")
    ex = lax.axis_index("expert")
    y, z, c = dp // 8, (dp // 2) % 4, dp % 2
    zh, xx = ex // 4, ex % 4
    oc = 1 - c

    def at(dy, dz, core):
        return (((y + dy) % 4) * 8 + ((z + dz) % 4) * 2 + core, ex)

    sib = at(0, 0, oc)
    opp_e = (dp, (1 - zh) * 4 + xx)

    def along_x(d):
        return (dp, zh * 4 + (xx + d) % 4)

    sends = []

    def send(src, dst, rsem, dev, when=None):
        d = pltpu.make_async_remote_copy(
            src_ref=src, dst_ref=dst, send_sem=ssem.at[len(sends)], recv_sem=rsem,
            device_id=dev, device_id_type=MESH,
        )
        if when is None:
            d.start()
        else:
            pl.when(when)(d.start)
        sends.append((d, when))

    def got(dst, rsem):
        pltpu.make_async_remote_copy(
            src_ref=dst, dst_ref=dst, send_sem=ssem.at[0], recv_sem=rsem,
            device_id=sib, device_id_type=MESH,
        ).wait_recv()

    small = [
        pltpu.make_async_copy(a, b, lsem.at[5 + i])
        for i, (a, b) in enumerate(
            ((tokens_h, tokens), (routes_h, routes), (gates_h, gates), (saved_h, saved))
        )
    ]
    for d in small:
        d.start()
    states = [
        pltpu.make_async_copy(a, b, lsem.at[9 + i])
        for i, (a, b) in enumerate(((master_h, master), (moment_h, moment), (second_h, second)))
    ]
    grad_copy = pltpu.make_async_copy(grad_new, grad_h, lsem.at[12])

    bar = pltpu.get_barrier_semaphore()

    def greet(s, carry):
        pl.semaphore_signal(bar, inc=1, device_id=((dp + s) % 32, ex), device_id_type=MESH)
        return carry

    lax.fori_loop(1, 32, greet, 0)
    for dev in (opp_e, along_x(1), along_x(2), along_x(3)):
        pl.semaphore_signal(bar, inc=1, device_id=dev, device_id_type=MESH)

    local = [
        pltpu.make_async_copy(cot.at[c], cots.at[pl.ds(0, 64)], lsem.at[0]),
        pltpu.make_async_copy(w_rest, w.at[:, pl.ds(96, 6048)], lsem.at[1]),
        pltpu.make_async_copy(w_down.at[pl.ds(c * HALF, HALF)], wd.at[0], lsem.at[2]),
    ]
    local[0].start()
    for d in small:
        d.wait()
    tok_half[0] = tokens[:, :HALF].astype(F32)
    tok_half[1] = tokens[:, HALF:].astype(F32)
    lane = lax.broadcasted_iota(jnp.int32, (2, 128), 1)
    base = ex * 16 + c * 8
    route_row = jnp.zeros((2, 128), F32)
    gate_row = jnp.zeros((2, 128), F32)
    for t in range(8):
        here = lane == base + t
        route_row = jnp.where(here, routes[:, t : t + 1].astype(F32), route_row)
        gate_row = jnp.where(here, gates[:, t : t + 1], gate_row)
    meta_own[...] = jnp.zeros((8, 128), F32)
    meta_own[0:2, :] = route_row
    meta_own[2:4, :] = gate_row

    pl.semaphore_wait(bar, 35)

    send(tok_half.at[oc], tok_pair.at[c], s_pair.at[0], sib)
    send(meta_own, meta_sib, s_pair.at[1], sib)
    send(saved, saved_sib, s_pair.at[2], sib)
    send(cot.at[oc], cots.at[pl.ds(64, 64)], s_pair.at[3], sib)

    tok_pair[c] = tok_half[c]
    got(tok_pair.at[oc], s_pair.at[0])
    got(meta_sib, s_pair.at[1])
    meta_all[ex] = meta_own[...] + meta_sib[...]
    send(meta_all.at[ex], meta_all.at[ex], s_meta.at[1, 0], opp_e)
    for d in (1, 3, 2):
        send(meta_all.at[ex], meta_all.at[ex], s_meta.at[0, (4 - d) % 4], along_x(d))

    def tokens_zh(q):
        send(toks.at[q, ex], toks.at[q, ex], s_tok.at[q, 1, 0], opp_e)

    for q in range(Q):
        toks[q, ex] = tok_pair[:, :, q * W : (q + 1) * W].reshape(16, W).astype(BF)
        if q == 0:
            tokens_zh(0)
        for d in (1, 3, 2):
            send(toks.at[q, ex], toks.at[q, ex], s_tok.at[q, 0, (4 - d) % 4], along_x(d))

    got(saved_sib, s_pair.at[2])
    saved_t[...] = jnp.transpose(
        jnp.concatenate([saved[...].astype(F32), saved_sib[...].astype(F32)], axis=0)
    ).astype(BF)
    local[0].wait()
    tokens_zh(1)
    got(cots.at[pl.ds(64, 64)], s_pair.at[3])
    for dy in (2, 1, 3, 0):
        for h in range(2):
            cols = pl.ds(pl.multiple_of(((y + dy) % 4) * 2048 + h * 1024, 1024), 1024)
            pg[dy, h] = jnp.dot(saved_t[...], cots[:, cols], preferred_element_type=F32).astype(BF)
        if dy == 2:
            send(pg.at[2, 0], g_opp.at[0], s_gopp.at[0], at(3, 0, c))
            send(pg.at[2, 1], g_opp.at[1], s_gopp.at[1], at(1, 0, c))
            tokens_zh(2)
        if dy == 1:
            send(pg.at[1, 0], g_fin.at[0, 0], s_gfin.at[0, 0], at(1, 0, c))
        if dy == 3:
            send(pg.at[3, 1], g_fin.at[1, 1], s_gfin.at[1, 1], at(3, 0, c))

    local[1].start()
    local[2].start()
    send(w_down.at[pl.ds(oc * HALF, HALF)], wd.at[1], s_pair.at[4], sib)
    for d in states:
        d.start()

    other = (1 - zh) * 4 + xx
    got(meta_all.at[other], s_meta.at[1, 0])
    for d in (1, 3, 2):
        send(meta_all.at[other], meta_all.at[other], s_meta.at[1, (4 - d) % 4], along_x(d))
    for q in range(Q):
        got(toks.at[q, other], s_tok.at[q, 1, 0])
        for d in (1, 3, 2):
            send(toks.at[q, other], toks.at[q, other], s_tok.at[q, 1, (4 - d) % 4], along_x(d))

    got(g_opp.at[0], s_gopp.at[0])
    pg[3, 0] = (pg[3, 0].astype(F32) + g_opp[0].astype(F32)).astype(BF)
    send(pg.at[3, 0], g_fin.at[1, 0], s_gfin.at[1, 0], at(3, 0, c))
    got(g_opp.at[1], s_gopp.at[1])
    pg[1, 1] = (pg[1, 1].astype(F32) + g_opp[1].astype(F32)).astype(BF)
    send(pg.at[1, 1], g_fin.at[0, 1], s_gfin.at[0, 1], at(1, 0, c))

    for d in (1, 3, 2):
        for k in range(2):
            src = (zh if k == 0 else 1 - zh) * 4 + (xx + d) % 4
            got(meta_all.at[src], s_meta.at[k, d])
    meta = meta_all[0]
    for e in range(1, 8):
        meta = meta + meta_all[e]
    mine = ex.astype(F32)
    first = meta[0:1, :] == mine
    hit = jnp.logical_or(first, meta[1:2, :] == mine)
    hit_f = jnp.where(hit, 1.0, 0.0).astype(F32)
    gate_of = jnp.where(first, meta[2:3, :], meta[3:4, :])
    before = jnp.where(
        lax.broadcasted_iota(jnp.int32, (128, 128), 0)
        < lax.broadcasted_iota(jnp.int32, (128, 128), 1),
        1.0,
        0.0,
    ).astype(BF)
    rank = jnp.dot(
        jnp.broadcast_to(hit_f, (16, 128)).astype(BF), before, preferred_element_type=F32
    )[0:1, :]
    slot_id = lax.broadcasted_iota(jnp.int32, (ROWS, 128), 0).astype(F32)
    chosen = jnp.where(slot_id == rank, 1.0, 0.0).astype(F32) * hit_f
    row_gate = jnp.sum(chosen * gate_of, axis=1, keepdims=True)
    pick[0] = chosen
    pick[1] = jnp.broadcast_to(row_gate, (ROWS, 128))

    def pass_block(q, dy, s, y_sides):
        for side in y_sides:
            to = (dy - side) % 4
            send(x.at[0, q, dy, s], x.at[0, q, to, s], s_x.at[q, to, s], at(side, 0, c))
        send(x.at[0, q, dy, s], x.at[1, q, dy, s], s_xs.at[q, dy, s], sib)

    def own_along_z(q):
        for s in (1, 2, 3):
            t = SLOT[(4 - DZ[s]) % 4]
            near_by = None if s == 3 else (z < 3 if s == 1 else z > 0)
            send(x.at[0, q, 0, 0], x.at[0, q, 0, t], s_x.at[q, 0, t], at(0, DZ[s], c), near_by)

    def on_along_z(q):
        send(x.at[0, q, 0, 3], x.at[0, q, 0, 1], s_x.at[q, 0, 1], at(0, 1, c), z == 2)
        send(x.at[0, q, 0, 3], x.at[0, q, 0, 2], s_x.at[q, 0, 2], at(0, 3, c), z == 1)

    for q in range(Q):
        for d in (1, 3, 2):
            for k in range(2):
                src = (zh if k == 0 else 1 - zh) * 4 + (xx + d) % 4
                got(toks.at[q, src], s_tok.at[q, k, d])
        x[0, q, 0, 0] = jnp.dot(
            pick[0].astype(BF), toks[q].reshape(128, W), preferred_element_type=F32
        ).astype(BF)
        if q == 0:
            own_along_z(0)
            pass_block(0, 0, 0, (1, 3))

    for h in range(2):
        got(g_fin.at[0, h], s_gfin.at[0, h])
        got(g_fin.at[1, h], s_gfin.at[1, h])
        total = pg[0, h].astype(F32) + g_fin[0, h].astype(F32) + g_fin[1, h].astype(F32)
        zg[2 * h] = total[:, :512].astype(BF)
        zg[2 * h + 1] = total[:, 512:].astype(BF)
    for d in (1, 3, 2):
        send(zg.at[(z + d) % 4], zg_in.at[3 - d], s_zg.at[3 - d], at(0, d, c))

    for q in range(1, Q):
        pass_block(q, 0, 0, (1, 3))

    def wide(p):
        return pl.ds(pl.multiple_of((p // 2) * 512, 512), 512)

    def narrow(p):
        return pl.ds(pl.multiple_of(p * UNITS, UNITS), UNITS)

    def exchange(src_of, dst_of, wait_of, out_sem, in_sem):
        def copy_to(s):
            p = (dp + s) % 32
            return pltpu.make_async_remote_copy(
                src_ref=src_of(p), dst_ref=dst_of(dp), send_sem=out_sem.at[s],
                recv_sem=in_sem.at[dp], device_id=(p, ex), device_id_type=MESH,
            )

        def start(s, carry):
            copy_to(s).start()
            return carry

        def finish(s, carry):
            p = (dp + s) % 32
            pltpu.make_async_remote_copy(
                src_ref=src_of(p), dst_ref=dst_of(p), send_sem=out_sem.at[s],
                recv_sem=in_sem.at[p], device_id=(p, ex), device_id_type=MESH,
            ).wait_recv()
            return carry

        def sent(s, carry):
            copy_to(s).wait_send()
            return carry

        def begin():
            pltpu.make_async_copy(src_of(dp), dst_of(dp), lsem.at[wait_of]).start()
            lax.fori_loop(1, 32, start, 0)

        def arrive():
            pltpu.make_async_copy(src_of(dp), dst_of(dp), lsem.at[wait_of]).wait()
            lax.fori_loop(1, 32, finish, 0)

        return begin, arrive, lambda: lax.fori_loop(1, 32, sent, 0)

    to_rows, rows_here, rows_sent = exchange(
        lambda p: grad_out.at[pl.ds(p * 3, 3)], lambda p: grad.at[p % 2, :, :, wide(p)],
        3, s_ga, s_gb,
    )
    to_cols, cols_here, cols_sent = exchange(
        lambda p: bucket_out.at[:, :, narrow(p)], lambda p: bucket_in.at[pl.ds(p * 3, 3)],
        4, s_ba, s_bb,
    )

    def gradient_z():
        full = zg[z].astype(F32)
        for d in range(3):
            got(zg_in.at[d], s_zg.at[d])
            full = full + zg_in[d].astype(F32)
        grad_out[...] = full.reshape(96, 1, 512)
        to_rows()

    def adam():
        rows_here()
        for d in states:
            d.wait()

        def step(k, carry):
            cols = pl.ds(pl.multiple_of(k * 1024, 1024), 1024)
            g = jnp.concatenate([grad[0, :, :, cols], grad[1, :, :, cols]], axis=1)
            grad_new[:, :, cols] = g
            mo = beta_one * moment[:, :, cols] + (1.0 - beta_one) * g
            se = beta_two * second[:, :, cols] + (1.0 - beta_two) * g * g
            ma = master[:, :, cols] - rate * (mo / bias_one) / (jnp.sqrt(se / bias_two) + epsilon)
            bucket_out[:, :, cols] = ma.astype(BF).astype(F32)
            return carry

        lax.fori_loop(0, 8, step, 0)
        to_cols()
        grad_copy.start()

    def bucket_rows():
        cols_here()
        for m in range(2):
            w[m, 0:96, :] = bucket_in[:, m : m + 1, :].reshape(96, UNITS).astype(BF)

    def gate_up(q, dy):
        for s in range(4):
            got(x.at[1, q, dy, s], s_xs.at[q, dy, s])
        for hr in range(2):
            left = x[hr, q, dy].reshape(4 * ROWS, W)
            start = pl.multiple_of((c if hr == 0 else oc) * HALF + q * W, W)
            for m in range(2):
                part = jnp.dot(left, w[m, pl.ds(start, W), :], preferred_element_type=F32)
                if q == 0 and hr == 0:
                    acc[dy, m] = part
                else:
                    acc[dy, m] = acc[dy, m] + part

    def hidden(dy):
        left = jnp.where(c == 0, x[0, 0, dy, :, :, 0:128], x[1, 0, dy, :, :, 0:128]).reshape(
            4 * ROWS, 128
        )[:, 0:96]
        gate = acc[dy, 0] + jnp.dot(left, w[0, 0:96, :], preferred_element_type=F32)
        up = acc[dy, 1] + jnp.dot(left, w[1, 0:96, :], preferred_element_type=F32)
        hid[0, dy] = (gate / (1.0 + jnp.exp(-gate)) * up).astype(BF)
        send(hid.at[0, dy], hid.at[1, dy], s_hid.at[dy], sib)

    def down(q, dy):
        nt = (((1,), (1,)), ((), ()))
        rows = slice(STARTS[q], STARTS[q] + WIDTHS[q])
        out = lax.dot_general(hid[0, dy], wd[0, rows, :], nt, preferred_element_type=F32)
        out = out + lax.dot_general(hid[1, dy], wd[1, rows, :], nt, preferred_element_type=F32)
        po[q][dy] = out.astype(BF).reshape(4, ROWS, WIDTHS[q])

    A, B = pl.ds(0, 2), pl.ds(2, 2)

    near = jnp.where(z == 3, 2, 1)
    order = (3, near, 3 - near)

    def from_sides(q, k):
        in_a = k < 2
        s = 0 if k == 0 else order[k - 1]
        got(x.at[0, q, 3, s], s_x.at[q, 3, s])
        pass_block(q, 3, s, (1,) if in_a else ())
        got(x.at[0, q, 1, s], s_x.at[q, 1, s])
        pass_block(q, 1, s, () if in_a else (3,))

    def from_opposite(q):
        for s in (0, near, 3, 3 - near):
            got(x.at[0, q, 2, s], s_x.at[q, 2, s])
            pass_block(q, 2, s, ())

    for m in range(2):
        w[m, 0:96, :] = jnp.zeros((96, UNITS), BF)
    for q in range(Q):
        if q > 0:
            for s in (1, 2, 3):
                from_sides(q - 1, s)
        from_sides(q, 0)
        if q == 0:
            own_along_z(1)
        if q == 1:
            gradient_z()
        if q == 2:
            adam()
        for k in range(3):
            s = order[k]
            got(x.at[0, q, 0, s], s_x.at[q, 0, s])
            if k == 0:
                on_along_z(q)
            pass_block(q, 0, s, (1, 3))
            if k == 1 and q + 2 < Q:
                own_along_z(q + 2)
        if q == 0:
            local[1].wait()
        gate_up(q, 0)
        if q > 0:
            gate_up(q - 1, 1)
            gate_up(q - 1, 3)
            from_opposite(q - 1)
            gate_up(q - 1, 2)
    for s in (1, 2, 3):
        from_sides(Q - 1, s)
    gate_up(2, 1)
    gate_up(2, 3)
    bucket_rows()
    hidden(1)
    hidden(3)
    local[2].wait()
    got(wd.at[1], s_pair.at[4])

    def direct(q):
        send(po[q].at[1, A], r_fin[q].at[0, A], s_rfin.at[q, 0, 0], at(1, 0, c))
        send(po[q].at[3, B], r_fin[q].at[1, B], s_rfin.at[q, 1, 1], at(3, 0, c))

    def opposite(q):
        send(po[q].at[2, A], r_opp[q].at[0], s_ropp.at[q, 0], at(3, 0, c))
        send(po[q].at[2, B], r_opp[q].at[1], s_ropp.at[q, 1], at(1, 0, c))

    def add_opposite(q):
        got(r_opp[q].at[0], s_ropp.at[q, 0])
        po[q][3, 0:2] = (po[q][3, 0:2].astype(F32) + r_opp[q][0].astype(F32)).astype(BF)
        send(po[q].at[3, A], r_fin[q].at[1, A], s_rfin.at[q, 1, 0], at(3, 0, c))
        got(r_opp[q].at[1], s_ropp.at[q, 1])
        po[q][1, 2:4] = (po[q][1, 2:4].astype(F32) + r_opp[q][1].astype(F32)).astype(BF)
        send(po[q].at[1, B], r_fin[q].at[0, B], s_rfin.at[q, 0, 1], at(1, 0, c))

    def direct_here(q):
        got(r_fin[q].at[0, A], s_rfin.at[q, 0, 0])
        got(r_fin[q].at[1, B], s_rfin.at[q, 1, 1])

    def along_z(q):
        def y_sum(s):
            return po[q][0, s].astype(F32) + r_fin[q][0, s].astype(F32) + r_fin[q][1, s].astype(F32)

        def pass_on(s):
            z_out[q][s - 1] = y_sum(s).astype(BF)
            t = SLOT[(4 - DZ[s]) % 4] - 1
            send(z_out[q].at[s - 1], rz[q].at[t], s_rz.at[q, t], at(0, DZ[s], c))

        got(r_fin[q].at[1, A], s_rfin.at[q, 1, 0])
        pass_on(1)
        got(r_fin[q].at[0, B], s_rfin.at[q, 0, 1])
        pass_on(3)
        pass_on(2)
        z_own[q][...] = y_sum(0)

    def place_rows(q):
        total = z_own[q][...]
        for s in range(3):
            got(rz[q].at[s], s_rz.at[q, s])
            total = total + rz[q][s].astype(F32)
        scaled = (total * pick[1][:, 0:1]).astype(BF)
        placed = lax.dot_general(
            pick[0].astype(BF), scaled, (((0,), (0,)), ((), ())), preferred_element_type=F32
        )
        ct[q][...] = placed.astype(BF).reshape(2, 4, 16, WIDTHS[q])
        for d in (1, 3, 2):
            send(ct[q].at[:, (xx + d) % 4], rx[q].at[3 - d], s_rx.at[q, 3 - d], along_x(d))

    def x_sum(q, which):
        total = ct[q][which, xx].astype(F32)
        for d in range(3):
            total = total + rx[q][d, which].astype(F32)
        return total

    def along_zh(q):
        for d in range(3):
            got(rx[q].at[d], s_rx.at[q, d])
        zh_out[q][...] = x_sum(q, 1 - zh).astype(BF)
        send(zh_out[q], zh_in[q], s_zh.at[q], opp_e)
        own_out[q][...] = x_sum(q, zh).reshape(2, 8, WIDTHS[q])

    def halves(q):
        got(zh_in[q], s_zh.at[q])
        own_out[q][...] = own_out[q][...] + zh_in[q][...].astype(F32).reshape(2, 8, WIDTHS[q])
        send(own_out[q].at[oc], own_in[q], s_fin.at[q], sib)

    def finish_rows(q):
        def put(core, value):
            start = pl.multiple_of(core * HALF + STARTS[q], 128)
            mixed[:, pl.ds(start, WIDTHS[q])] = value.astype(BF)

        put(c, own_out[q][c])
        got(own_in[q], s_fin.at[q])
        put(oc, own_in[q][...])

    for dy in (1, 3):
        got(hid.at[1, dy], s_hid.at[dy])
        down(0, dy)
    direct(0)
    for dy in (1, 3):
        down(1, dy)
    from_opposite(2)
    direct(1)
    gate_up(2, 2)
    hidden(2)
    hidden(0)
    got(hid.at[1, 2], s_hid.at[2])
    down(0, 2)
    opposite(0)
    down(1, 2)
    opposite(1)
    got(hid.at[1, 0], s_hid.at[0])
    down(0, 0)
    for r in range(R):
        if r + 2 < R:
            down(r + 2, 2)
        add_opposite(r)
        if r + 2 < R:
            opposite(r + 2)
            down(r + 2, 1)
            down(r + 2, 3)
        direct_here(r)
        if r + 2 < R:
            direct(r + 2)
        if r + 1 < R:
            down(r + 1, 0)
        if r >= 1:
            along_z(r - 1)
        if r >= 2:
            place_rows(r - 2)
        if r >= 3:
            along_zh(r - 3)
    along_z(R - 1)
    place_rows(R - 2)
    along_zh(R - 3)
    for r in range(R - 3):
        halves(r)
    place_rows(R - 1)
    along_zh(R - 2)
    halves(R - 3)
    for r in range(R - 3):
        finish_rows(r)
    along_zh(R - 1)
    halves(R - 2)
    finish_rows(R - 3)
    finish_rows(R - 2)
    halves(R - 1)
    finish_rows(R - 1)

    for d, when in sends:
        if when is None:
            d.wait_send()
        else:
            pl.when(when)(d.wait_send)
    rows_sent()
    cols_sent()
    grad_copy.wait()


def body(tokens, routes, gates, saved_inputs, cotangents, master, moment, second, w_rest, w_down):
    cot = jnp.transpose(cotangents[0, 0], (1, 0, 2))
    rows = [jnp.swapaxes(a[0], 0, 1) for a in (master, moment, second)]
    vmem = pl.BlockSpec(memory_space=pltpu.VMEM)
    hbm = pl.BlockSpec(memory_space=pl.ANY)
    dma = pltpu.SemaphoreType.DMA
    mem = pltpu.VMEM
    mixed, gradient = pl.pallas_call(
        kernel,
        out_shape=(jax.ShapeDtypeStruct((8, D), BF), jax.ShapeDtypeStruct((3, 2, 8192), F32)),
        in_specs=[hbm] * 10,
        out_specs=(vmem, hbm),
        scratch_shapes=[
            mem((8, D), BF),
            mem((2, 8), jnp.int32),
            mem((2, 8), F32),
            mem((64, 96), BF),
            mem((3, 2, 8192), F32),
            mem((3, 2, 8192), F32),
            mem((3, 2, 8192), F32),
            mem((3, 2, 8192), F32),
            mem((2, 8, HALF), F32),
            mem((2, 8, HALF), F32),
            mem((8, 128), F32),
            mem((8, 128), F32),
            mem((8, 8, 128), F32),
            mem((Q, 8, 16, W), BF),
            mem((64, 96), BF),
            mem((96, 128), BF),
            mem((128, 8192), BF),
            mem((4, 2, 96, 1024), BF),
            mem((2, 96, 1024), BF),
            mem((2, 2, 96, 1024), BF),
            mem((4, 96, 512), BF),
            mem((3, 96, 512), BF),
            mem((96, 1, 512), F32),
            mem((2, 3, 1, 8192), F32),
            mem((3, 2, 8192), F32),
            mem((96, 2, UNITS), F32),
            mem((2, D, UNITS), BF),
            mem((2, HALF, UNITS), BF),
            mem((2, ROWS, 128), F32),
            mem((2, Q, 4, 4, ROWS, W), BF),
            mem((2, 4, 4 * ROWS, UNITS), BF),
            mem((4, 2, 4 * ROWS, UNITS), F32),
            [mem((4, 4, ROWS, v), BF) for v in WIDTHS],
            [mem((2, 2, ROWS, v), BF) for v in WIDTHS],
            [mem((2, 4, ROWS, v), BF) for v in WIDTHS],
            [mem((3, ROWS, v), BF) for v in WIDTHS],
            [mem((ROWS, v), F32) for v in WIDTHS],
            [mem((3, ROWS, v), BF) for v in WIDTHS],
            [mem((2, 4, 16, v), BF) for v in WIDTHS],
            [mem((3, 2, 16, v), BF) for v in WIDTHS],
            [mem((16, v), BF) for v in WIDTHS],
            [mem((16, v), BF) for v in WIDTHS],
            [mem((2, 8, v), F32) for v in WIDTHS],
            [mem((8, v), F32) for v in WIDTHS],
            dma((N_SEND,)), dma((13,)), dma((5,)), dma((Q, 2, 4)), dma((2, 4)),
            dma((Q, 4, 4)), dma((Q, 4, 4)), dma((2,)), dma((2, 2)), dma((3,)),
            dma((32,)), dma((32,)), dma((32,)), dma((32,)),
            dma((4,)), dma((R, 2)), dma((R, 2, 2)), dma((R, 3)), dma((R, 3)), dma((R,)), dma((R,)),
        ],
        compiler_params=pltpu.CompilerParams(
            collective_id=0, has_side_effects=True, vmem_limit_bytes=60 * 1024 * 1024
        ),
        cost_estimate=pl.CostEstimate(flops=8 * 10**9, bytes_accessed=12 * 10**6, transcendentals=0),
    )(
        tokens, jnp.transpose(routes), jnp.transpose(gates), saved_inputs[0, 0], cot, *rows,
        w_rest[0], w_down[0],
    )
    gradient = jnp.swapaxes(gradient, 0, 1)[None]
    moment_new = beta_one * moment + (1.0 - beta_one) * gradient
    second_new = beta_two * second + (1.0 - beta_two) * gradient * gradient
    master_new = master - rate * (moment_new / bias_one) / (
        jnp.sqrt(second_new / bias_two) + epsilon
    )
    return (mixed, master_new, moment_new, second_new)


def solution(mesh):
    in_specs = (
        P(("dp", "expert"), None),
        P(("dp", "expert"), None),
        P(("dp", "expert"), None),
        P("dp", "expert", None, None),
        P("dp", "expert", None, None, None),
        P("expert", None, "dp", None),
        P("expert", None, "dp", None),
        P("expert", None, "dp", None),
        P("expert", None, None, "dp"),
        P("expert", None, "dp"),
    )
    out_specs = (
        P(("dp", "expert"), None),
        P("expert", None, "dp", None),
        P("expert", None, "dp", None),
        P("expert", None, "dp", None),
    )
    return jax.shard_map(body, mesh=mesh, in_specs=in_specs, out_specs=out_specs, check_vma=False)
```
